128 devices in a mesh: lat: 8 (over y, core), lon: 16 (over x, z).
Axes of the slice: x: 4, y: 4, z: 4, core: 2. Of those that a mesh axis runs over, the one named last changes fastest.
Arguments:
- fields: bfloat16 [80, 512, 2048], P(None, 'lat', 'lon'), may hold values from -6 to 6
- depart_lists: int32 [128, 16, 2], P('lat', 'lon'), may hold values from 0 to 2047, as said below
- stencil_offsets: int32 [512, 2048], P('lat', 'lon'), may hold values from 0 to 4
- interp_weights: float32 [4, 512, 2048], P(None, 'lat', 'lon'), may hold values from -0.07 to 1
- diag_coef: float32 [512, 2048], P('lat', 'lon'), may hold values from 0.05 to 2
- level_scale: float32 [16], replicated, may hold values from 0.5 to 4
Outputs:
- advected: bfloat16 [64, 512, 2048], P(None, 'lat', 'lon')
- pressure: float32 [16, 512, 2048], P(None, 'lat', 'lon')
- residual: float32 [16, 512, 2048], P(None, 'lat', 'lon')
The draws below stay inside these ranges and needn't reach their ends.
Inputs may be any that keep to these rules, and one draw needn't show every extreme that they name: `depart_lists`: the entries of a reader device name tiles of its own band or the bands next to it, and of its own sector, the two sectors next to it (periodic in longitude), or, for devices of the first and last band only, the sector across the pole (own sector + 8, counted round); every such polar device names that sector at least once. Among the 32 entries of one device, exactly 16 name tiles of one sector, and each other sector is named fewer than 16 times.
All inputs are finite; a program needn't handle non-finite values.
Results may differ from the reference program's by a relative error of at most 0.0004.
Values may be sent and summed in bfloat16 or wider, within the bound.
No kernel may reach another device: no remote copies, remote signals or barrier semaphores. Data moves between devices by JAX's collectives and lax.ppermute only.
A program may use at most 128 MiB of HBM per device.

```python
import math
import jax
import jax.numpy as jnp
from jax import lax

LEV = 16
TILE_ROWS = 4
SOURCES = 2
ITERS = 2
COLS = 128
FL = 80
TILES = 16
NROWS = 512
NCOLS = 2048
N_LAT = 8
N_LON = 16


def draw_depart_lists(key, part):
    key = jax.random.fold_in(key, 11)
    device_count = N_LAT * N_LON
    slot_count = TILES * SOURCES
    half_count = slot_count // 2

    def one_reader(reader_key, device):
        key_hot, key_near, key_far, key_perm, key_band, key_local = jax.random.split(reader_key, 6)
        band_here = device // N_LON
        sector_here = device % N_LON
        polar = jnp.logical_or(band_here == 0, band_here == N_LAT - 1)
        hot_pick = jax.random.randint(key_hot, (), 0, 3)
        near_pick = jax.random.randint(key_near, (slot_count - half_count,), 0, 2)
        far_pick = jax.random.randint(key_far, (slot_count - half_count,), 0, 3)
        other_pick = jnp.where(polar, far_pick, near_pick)
        other_pick = other_pick.at[0].set(jnp.where(polar, 2, other_pick[0]))
        other_rel = jnp.where(other_pick == 2, 3, (hot_pick + 1 + other_pick) % 3)
        rel = jnp.concatenate([jnp.full((half_count,), hot_pick, jnp.int32), other_rel.astype(jnp.int32)])
        rel = jax.random.permutation(key_perm, rel)
        sector = jnp.where(rel == 3, sector_here + N_LON // 2, sector_here + rel - 1 + N_LON) % N_LON
        band_step = jax.random.randint(key_band, (slot_count,), -1, 2)
        band = jnp.clip(band_here + band_step, 0, N_LAT - 1)
        local_ids = jax.random.randint(key_local, (slot_count,), 0, TILES)
        return ((band * N_LON + sector) * TILES + local_ids).astype(jnp.int32)
    devices = jnp.arange(device_count, dtype=jnp.int32)
    ids = jax.vmap(one_reader)(jax.random.split(key, device_count), devices)
    ids = ids.reshape(N_LAT, N_LON, TILES, SOURCES).transpose(0, 2, 1, 3)
    return ids.reshape(N_LAT * TILES, N_LON, SOURCES)


def draw_interp_weights(key, part):
    key = jax.random.fold_in(key, 23)
    uniform_draw = jax.random.uniform(key, (NROWS, NCOLS), jnp.float32)
    fraction = uniform_draw
    first = -fraction * (fraction - 1.0) * (fraction - 2.0) / 6.0
    second = (fraction + 1.0) * (fraction - 1.0) * (fraction - 2.0) / 2.0
    third = -(fraction + 1.0) * fraction * (fraction - 2.0) / 2.0
    fourth = (fraction + 1.0) * fraction * (fraction - 1.0) / 6.0
    return jnp.stack([first, second, third, fourth]).astype(jnp.float32)


def set_ends(values, key, low, high):
    spot = [jax.random.randint(jax.random.fold_in(key, axis), (), 0, length) for axis, length in enumerate(values.shape)]
    longest = values.shape.index(max(values.shape))
    beside = spot[:longest] + [(spot[longest] + 1) % values.shape[longest]] + spot[longest + 1:]
    return values.at[tuple(spot)].set(low).at[tuple(beside)].set(high)


def block_scale(rng, dims, shards, smallest, high):
    factor_of, own = 1.0, jax.random.fold_in(rng, 6)
    for dim, parts in shards:
        steps = jnp.exp(jax.random.uniform(jax.random.fold_in(own, dim), (parts,), jnp.float32, smallest / len(shards), high / len(shards)))
        factor_of = factor_of * jnp.repeat(steps, dims[dim] // parts).reshape([-1 if axis == dim else 1 for axis in range(len(dims))])
    return factor_of


def gaussian(own_key, extent, spread, reach, cuts=(), kind=jnp.bfloat16):
    entries = jax.random.normal(own_key, extent, jnp.float32) * spread
    if len(cuts) > 0:
        entries = block_scale(own_key, extent, cuts, -0.22, 0.18) * entries
    return jnp.clip(entries, min=-reach, max=reach).astype(kind)


def setup_inputs(seed: int = 0) -> dict:
    key_of = jax.random.split(jax.random.key(seed), 7)
    return {
        "fields": gaussian(key_of[0], (FL, NROWS, NCOLS), 1.0, 6.0, ((1, 8), (2, 16))),
        "depart_lists": draw_depart_lists(jax.random.fold_in(key_of[6], 71), 0),
        "stencil_offsets": set_ends(jax.random.randint(key_of[2], (NROWS, NCOLS), 0, SOURCES * TILE_ROWS - 3), jax.random.fold_in(key_of[2], 1), 0, (SOURCES * TILE_ROWS - 3) - 1).astype(jnp.int32),
        "interp_weights": draw_interp_weights(jax.random.fold_in(key_of[6], 71), 0),
        "diag_coef": jnp.clip(jnp.exp(math.log(2.0) - 3.6888794 * jax.random.uniform(key_of[4], (NROWS, NCOLS), jnp.float32) ** block_scale(key_of[4], (NROWS, NCOLS), ((0, 8), (1, 16)), -0.2, 0.2)), 0.05, 2.0),
        "level_scale": jnp.clip(jnp.exp(jax.random.uniform(key_of[5], (LEV,), jnp.float32, math.log(0.5), math.log(4.0))), 0.5, 4.0),
    }


def operate(field, coef):
    padded = jnp.pad(field, ((0, 0), (1, 1), (0, 0)))
    beside = padded[:, 2:, :] + padded[:, :-2, :]
    beside = beside + jnp.roll(field, 1, axis=2) + jnp.roll(field, -1, axis=2)
    return coef * field - beside


def level_inner(first, second):
    return jnp.sum(first * second, axis=(1, 2))


def reference(fields, depart_lists, stencil_offsets, interp_weights, diag_coef, level_scale):
    tile_rows_all = TILES * N_LAT
    offsets = stencil_offsets.reshape(tile_rows_all, TILE_ROWS, N_LON, COLS).transpose(0, 2, 1, 3).astype(jnp.int32)
    weights = interp_weights.reshape(4, tile_rows_all, TILE_ROWS, N_LON, COLS).transpose(0, 1, 3, 2, 4)

    def one_field(plane):
        blocks = plane.reshape(N_LAT, TILES, TILE_ROWS, N_LON, COLS).transpose(0, 3, 1, 2, 4)
        blocks = blocks.reshape(N_LAT * N_LON * TILES, TILE_ROWS * COLS)
        source = jnp.take(blocks, depart_lists, axis=0).reshape(tile_rows_all, N_LON, SOURCES * TILE_ROWS, COLS)
        summed = jnp.zeros((tile_rows_all, N_LON, TILE_ROWS, COLS), jnp.float32)
        for point in range(4):
            picked = jnp.take_along_axis(source, offsets + point, axis=2)
            summed = summed + weights[point] * picked.astype(jnp.float32)
        return summed.transpose(0, 2, 1, 3).reshape(NROWS, NCOLS)

    interp = lax.map(one_field, fields)
    advected = interp[:4 * LEV].astype(jnp.bfloat16)
    rhs = interp[4 * LEV:] + 0.5 * interp[2 * LEV:3 * LEV]
    coef = 4.0 + diag_coef[None, :, :] * level_scale[:, None, None]
    pressure = jnp.zeros_like(rhs)
    residual = rhs
    smoothed = residual / coef
    direction = smoothed
    norm_now = level_inner(residual, smoothed)
    for sweep in range(ITERS):
        image = operate(direction, coef)
        step_size = norm_now / level_inner(direction, image)
        pressure = pressure + step_size[:, None, None] * direction
        residual = residual - step_size[:, None, None] * image
        if sweep + 1 < ITERS:
            smoothed = residual / coef
            norm_next = level_inner(residual, smoothed)
            direction = smoothed + (norm_next / norm_now)[:, None, None] * direction
            norm_now = norm_next
    return advected, pressure, residual
```

```python
import functools

import jax
import jax.numpy as jnp
from jax import lax
from jax.experimental import pallas as pl
from jax.experimental.pallas import tpu as pltpu
from jax.sharding import PartitionSpec as P

ROWS = 4
LANES = 128
SPAN = 64
F32 = jnp.float32
BF16 = jnp.bfloat16


def iota(shape, dim):
    return lax.broadcasted_iota(jnp.int32, shape, dim)


def ring(axis, step):
    count = lax.axis_size(axis)
    return [(i, (i + step) % count) for i in range(count)]


def line(axis, step):
    count = lax.axis_size(axis)
    return [(i, i + step) for i in range(count) if 0 <= i + step < count]


def across_pole():
    bands, sectors = lax.axis_size("lat"), lax.axis_size("lon")
    return [
        (band * sectors + s, band * sectors + (s + sectors // 2) % sectors)
        for band in (0, bands - 1)
        for s in range(sectors)
    ]


def to_lat(block, step):
    return lax.ppermute(block, "lat", line("lat", step))


def to_lon(block, step):
    return lax.ppermute(block, "lon", ring("lon", step))


def to_far(block):
    return lax.ppermute(block, ("lat", "lon"), across_pole())


def coded(depart_lists, tiles):
    sectors = lax.axis_size("lon")
    wanted = depart_lists.reshape(1, -1)
    owner = wanted // tiles
    turn = (owner % sectors - lax.axis_index("lon") + sectors) % sectors
    tile = (owner // sectors - lax.axis_index("lat") + 1) * tiles + wanted % tiles
    code = turn * SPAN + tile
    return jnp.pad(code, ((0, 0), (0, LANES - code.shape[1])), constant_values=2 * SPAN)


def ranks(member):
    before = (iota((LANES, LANES), 0) < iota((LANES, LANES), 1)).astype(BF16)
    ones = jnp.where(member, 1.0, 0.0).astype(BF16)
    return jnp.dot(ones, before, preferred_element_type=F32)


def pack_kernel(sectors, left, right, far, low, own, high, out_left, out_right, out_far, pick):
    @pl.when(pl.program_id(0) == 0)
    def _():
        sub = iota((8, LANES), 0)
        codes = jnp.where(sub == 0, left[...], jnp.where(sub == 1, right[...], far[...]))
        want = jnp.where(sub == 0, 1, jnp.where(sub == 1, sectors - 1, sectors // 2))
        member = (codes >> 6) == want
        rank = jnp.where(member, ranks(member), -1.0)
        tile = ((codes & (SPAN - 1)) + 1).astype(F32)
        slot = (iota((64, LANES), 0) >> 2).astype(F32)
        row = (iota((64, 192), 0) & 3).astype(F32)
        col = iota((64, 192), 1).astype(F32)
        for d in range(3):
            hit = rank[d : d + 1] == slot
            held = jnp.sum(jnp.where(hit, tile[d : d + 1], 0.0), axis=1, keepdims=True) - 1.0
            pick[d * 64 : (d + 1) * 64, :] = jnp.where(col == held * 4.0 + row, 1.0, 0.0).astype(BF16)

    def pair(g, carry):
        pool = jnp.concatenate(
            [jnp.concatenate([low[f], own[f], high[f]], axis=0) for f in (2 * g, 2 * g + 1)], axis=1
        )
        got = jnp.dot(pick[...], pool, preferred_element_type=F32).astype(BF16)
        for d, out in enumerate((out_left, out_right, out_far)):
            for half in range(2):
                out[2 * g + half] = got[d * 64 : (d + 1) * 64, half * LANES : (half + 1) * LANES]
        return carry

    lax.fori_loop(0, own.shape[0] // 2, pair, 0, unroll=4)


def pack(lists, bands, step):
    levels = bands[0].shape[0]
    sectors = lax.axis_size("lon")
    block = pl.BlockSpec((step, 64, LANES), lambda g: (g, 0, 0))
    row = pl.BlockSpec((1, LANES), lambda g: (0, 0))
    return pl.pallas_call(
        functools.partial(pack_kernel, sectors),
        grid=(levels // step,),
        in_specs=[row] * 3 + [block] * 3,
        out_specs=[block] * 3,
        out_shape=[jax.ShapeDtypeStruct((levels, 64, LANES), BF16)] * 3,
        scratch_shapes=[pltpu.VMEM((192, 192), BF16)],
        compiler_params=pltpu.CompilerParams(vmem_limit_bytes=32 << 20),
        cost_estimate=pl.CostEstimate(
            flops=levels * 2 * 192 * 192 * LANES, bytes_accessed=levels * 6 * 64 * LANES * 2, transcendentals=0
        ),
        name="pack",
    )(*lists, *bands)


def set_gather(sectors, codes_ref, gather):
    codes = jnp.broadcast_to(codes_ref[...], (8, LANES))
    turn = codes >> 6
    sub = iota((8, LANES), 0)
    group = jnp.where(sub == 1, sectors - 1, jnp.where(sub == 2, 1, jnp.where(sub == 3, sectors // 2, 0)))
    rank = ranks(turn == group)
    turn = turn[:1]
    place = jnp.where(turn == 0, (codes[:1] & (SPAN - 1)).astype(F32), -1.0)
    place = jnp.where(turn == sectors - 1, 48.0 + rank[1:2], place)
    place = jnp.where(turn == 1, 64.0 + rank[2:3], place)
    place = jnp.where(turn == sectors // 2, 80.0 + rank[3:4], place)
    row = iota((LANES, LANES), 0)
    mine = iota((LANES, LANES), 1) == 2 * (row & 15) + (row >> 6)
    place = jnp.sum(jnp.where(mine, place, 0.0), axis=1, keepdims=True)
    within = ((iota((LANES, 384), 0) >> 4) & 3).astype(F32)
    col = iota((LANES, 384), 1).astype(F32)
    gather[...] = jnp.where(col == place * 4.0 + within, 1.0, 0.0).astype(BF16)


def every_fourth(q):
    return pl.ds(q, 16, stride=4)


def set_weights(offsets, weights, coef):
    for q in range(4):
        offset = offsets[every_fourth(q), :]
        points = [weights[m, every_fourth(q), :] for m in range(4)]
        for r in range(8):
            value = jnp.zeros((16, LANES), F32)
            for m in range(4):
                if 0 <= r - m <= 4:
                    value = jnp.where(offset == r - m, points[m], value)
            coef[q * 8 + r] = value


def interpolate(gather, coef, pools, first, second):
    pool = jnp.concatenate(
        [jnp.concatenate([ref[f] for ref in pools], axis=0) for f in (first, second)], axis=1
    )
    rows = jnp.dot(gather[...], pool, preferred_element_type=F32)
    out = []
    for q in range(4):
        sums = [None, None]
        for r in range(8):
            weight = coef[q * 8 + r]
            for h in range(2):
                term = weight * rows[r * 16 : (r + 1) * 16, h * LANES : (h + 1) * LANES]
                sums[h] = term if r == 0 else sums[h] + term
        out.append(sums)
    return out


def first_kernel(
    sectors, scale, codes, offsets, weights, diag, low, own, high, left, right, far,
    adv, rhs, z, cols, up, down, gather, coef, tmp,
):
    set_gather(sectors, codes, gather)
    set_weights(offsets, weights, coef)
    pools = (low, own, high, left, right, far)

    def level(l, carry):
        values = interpolate(gather, coef, pools, l, 16 + l)
        for q in range(4):
            tmp[l, every_fourth(q), :] = values[q][0]
            rhs[l, every_fourth(q), :] = values[q][1] + 0.5 * values[q][0]
        return carry

    lax.fori_loop(0, 16, level, 0, unroll=2)
    group = iota((64, LANES), 1) >> 2
    packed = jnp.where(group == 16, pltpu.roll(diag[...], 65, 1), 0.0)
    for l in range(16):
        adv[l] = tmp[l].astype(BF16)
        value = rhs[l] / (4.0 + diag[...] * scale[l])
        z[l] = value
        packed = jnp.where(group == l, pltpu.roll(value, 2 + 4 * l, 1), packed)
        up[l : l + 1, :] = value[0:1]
        up[16 + l : 17 + l, :] = value[1:2]
        down[l : l + 1, :] = value[63:64]
        down[16 + l : 17 + l, :] = value[62:63]
    cols[...] = packed
    up[32:33, :] = diag[0:1, :]
    down[32:33, :] = diag[63:64, :]
    up[33:40, :] = jnp.ones((7, LANES), F32)
    down[33:40, :] = jnp.ones((7, LANES), F32)


SMEM = pl.BlockSpec(memory_space=pltpu.SMEM)
VMEM = pl.BlockSpec(memory_space=pltpu.VMEM)


def first_levels(scale, codes, offsets, weights, diag, pools):
    slab = jax.ShapeDtypeStruct((16, 64, LANES), F32)
    edge = jax.ShapeDtypeStruct((40, LANES), F32)
    whole = pl.BlockSpec((16, 64, LANES), lambda g: (0, 0, 0))
    flat = lambda rows: pl.BlockSpec((rows, LANES), lambda g: (0, 0))
    return pl.pallas_call(
        functools.partial(first_kernel, lax.axis_size("lon")),
        grid=(1,),
        in_specs=[SMEM] + [VMEM] * 10,
        out_specs=[
            pl.BlockSpec((16, 64, LANES), lambda g: (2, 0, 0)), whole, whole, flat(64), flat(40), flat(40)
        ],
        out_shape=[
            jax.ShapeDtypeStruct((64, 64, LANES), BF16), slab, slab,
            jax.ShapeDtypeStruct((64, LANES), F32), edge, edge,
        ],
        scratch_shapes=[
            pltpu.VMEM((LANES, 384), BF16), pltpu.VMEM((32, 16, LANES), F32), pltpu.VMEM((16, 64, LANES), F32)
        ],
        compiler_params=pltpu.CompilerParams(vmem_limit_bytes=32 << 20),
        cost_estimate=pl.CostEstimate(flops=32 * 2 * 128 * 384 * 128, bytes_accessed=6 << 20, transcendentals=0),
        name="first_levels",
    )(scale, codes, offsets, weights, diag, *pools)


def other_kernel(
    sectors, codes, offsets, weights, low, own, high, left, right, far, start, adv, gather, coef, tmp
):
    @pl.when(pl.program_id(0) == 0)
    def _():
        set_gather(sectors, codes, gather)
        set_weights(offsets, weights, coef)

    pools = (low, own, high, left, right, far)

    def pair(g, carry):
        values = interpolate(gather, coef, pools, 2 * g, 2 * g + 1)
        for h in range(2):
            for q in range(4):
                tmp[2 * g + h, every_fourth(q), :] = values[q][h]
        return carry

    count = own.shape[0]
    lax.fori_loop(0, count // 2, pair, 0, unroll=2)
    for f in range(count):
        adv[f] = tmp[f].astype(BF16)


def other_levels(codes, offsets, weights, pools, start):
    block = pl.BlockSpec((16, 64, LANES), lambda g: (g, 0, 0))
    flat = lambda rows: pl.BlockSpec((rows, LANES), lambda g: (0, 0))
    return pl.pallas_call(
        functools.partial(other_kernel, lax.axis_size("lon")),
        grid=(3,),
        in_specs=[flat(1), flat(64), pl.BlockSpec((4, 64, LANES), lambda g: (0, 0, 0))]
        + [block] * 6
        + [pl.BlockSpec(memory_space=pl.ANY)],
        out_specs=pl.BlockSpec((16, 64, LANES), lambda g: (g + g // 2, 0, 0)),
        out_shape=jax.ShapeDtypeStruct(start.shape, start.dtype),
        scratch_shapes=[
            pltpu.VMEM((LANES, 384), BF16), pltpu.VMEM((32, 16, LANES), F32), pltpu.VMEM((16, 64, LANES), F32)
        ],
        input_output_aliases={9: 0},
        compiler_params=pltpu.CompilerParams(vmem_limit_bytes=32 << 20),
        cost_estimate=pl.CostEstimate(flops=48 * 2 * 128 * 384 * 128, bytes_accessed=6 << 20, transcendentals=0),
        name="other_levels",
    )(codes, offsets, weights, *pools, start)


def sum_kernel(scale, z, rhs, diag, cols, left, right, above, below, n0, n1, sums, rowsums):
    lane = iota((64, LANES), 1)
    spread = jnp.zeros((1, LANES), F32)
    column = jnp.zeros((16, LANES), F32)
    for l in range(16):
        spread = jnp.where((lane[:1] >> 2) == l, scale[l], spread)
        column = jnp.where(iota((16, LANES), 0) == l, scale[l], column)
    row16, lane16 = iota((16, LANES), 0), lane[:16]

    def corner(row, which):
        return jnp.sum(jnp.where(lane16 == 4 * row16 + which, row, 0.0), axis=1, keepdims=True)

    def rim_row(edge, inner):
        near, second, flag = edge[0:16, :], edge[16:32, :], edge[33:34, :]
        west, east = corner(edge[34:35, :], 1), corner(edge[35:36, :], 2)
        beside = jnp.where(lane16 == 0, west, pltpu.roll(near, 1, 1))
        beside = beside + jnp.where(lane16 == LANES - 1, east, pltpu.roll(near, LANES - 1, 1))
        return flag * (second + inner + beside) / (4.0 + edge[32:33, :] * column)

    top_in = jnp.concatenate([z[l, 0:1, :] for l in range(16)], axis=0)
    low_in = jnp.concatenate([z[l, 63:64, :] for l in range(16)], axis=0)
    top, bottom = rim_row(above, top_in), rim_row(below, low_in)

    def rim_col(edge, first, last, toward, diag_lane):
        values = edge[...]
        up = jnp.concatenate([first, values[:-1]], axis=0)
        down = jnp.concatenate([values[1:], last], axis=0)
        outer = pltpu.roll(values, toward % LANES, 1)
        inner = pltpu.roll(cols[...], -toward % LANES, 1)
        coef = 4.0 + values[:, diag_lane : diag_lane + 1] * spread
        return (up + down + outer + inner) / coef

    west = rim_col(left, above[34:35, :], below[34:35, :], 1, 64)
    east = rim_col(right, above[35:36, :], below[35:36, :], -1, 65)

    def beside(value, west_col, east_col, upper, lower):
        total = jnp.where(lane == 0, west_col, pltpu.roll(value, 1, 1))
        total = total + jnp.where(lane == LANES - 1, east_col, pltpu.roll(value, LANES - 1, 1))
        total = total + jnp.concatenate([upper, value[:-1]], axis=0)
        return total + jnp.concatenate([value[1:], lower], axis=0)

    for l in range(16):
        value, start = z[l], rhs[l]
        inverse = 1.0 / (4.0 + diag[...] * scale[l])
        around = beside(
            value, left[:, 4 * l + 1 : 4 * l + 2], right[:, 4 * l + 2 : 4 * l + 3], above[l : l + 1, :], below[l : l + 1, :]
        )
        n0[l] = around
        again = around * inverse
        second = beside(
            again, west[:, 4 * l + 1 : 4 * l + 2], east[:, 4 * l + 2 : 4 * l + 3], top[l : l + 1], bottom[l : l + 1]
        )
        n1[l] = second
        for k, term in enumerate((start * value, start * again, around * again, second * again)):
            part = term[0:8]
            for j in range(1, 8):
                part = part + term[8 * j : 8 * j + 8]
            rowsums[k * 16 + l : k * 16 + l + 1, :] = jnp.sum(part, axis=0, keepdims=True)
    total = jnp.sum(rowsums[...], axis=1, keepdims=True)
    packed = jnp.zeros((8, LANES), F32)
    for j in range(8):
        packed = jnp.where(lane[:8] == j, total[8 * j : 8 * j + 8], packed)
    for j in range(sums.shape[0]):
        sums[j] = packed


def level_sums(scale, z, rhs, diag, cols, left, right, above, below):
    slab = jax.ShapeDtypeStruct((16, 64, LANES), F32)
    return pl.pallas_call(
        sum_kernel,
        in_specs=[SMEM] + [VMEM] * 8,
        out_specs=[VMEM] * 3,
        out_shape=[slab, slab, jax.ShapeDtypeStruct((lax.axis_size("lat"), 8, LANES), F32)],
        scratch_shapes=[pltpu.VMEM((64, LANES), F32)],
        compiler_params=pltpu.CompilerParams(vmem_limit_bytes=32 << 20),
        cost_estimate=pl.CostEstimate(flops=1 << 22, bytes_accessed=2 << 20, transcendentals=0),
        name="level_sums",
    )(scale, z, rhs, diag, cols, left, right, above, below)


def last_kernel(scale, parts, rhs, diag, n0, n1, pressure, residual):
    total = parts[0]
    for j in range(1, parts.shape[0]):
        total = total + parts[j]
    lane = iota((8, LANES), 1)

    def of(k, half):
        return jnp.sum(jnp.where(lane == 2 * k + half, total, 0.0), axis=1, keepdims=True)

    for half in range(2):
        s0, s1, s2, s3 = (of(k, half) for k in range(4))
        curve = s0 - s1
        step = s0 / curve
        keep = -s1 / curve
        norm = keep * keep * s0 + 2.0 * keep * step * s1 + step * step * s2
        ratio = norm / s0
        bend = norm - (keep * keep * s1 + 2.0 * keep * step * s2 + step * step * s3)
        other = norm / (bend - ratio * ratio * curve)
        along = other * (keep + ratio)
        across = other * step
        fit_z, fit_p = step + along, across
        fit_r, fit_n0, fit_n1 = keep - along, step + along - across, across
        for s in range(8):
            l = 8 * half + s
            at = lambda column: column[s : s + 1]
            inverse = 1.0 / (4.0 + diag[...] * scale[l])
            start, around = rhs[l], n0[l]
            pressure[l] = (at(fit_z) * start + at(fit_p) * around) * inverse
            residual[l] = at(fit_r) * start + at(fit_n0) * around + at(fit_n1) * n1[l]


def last_step(scale, parts, rhs, diag, n0, n1):
    slab = jax.ShapeDtypeStruct((16, 64, LANES), F32)
    return pl.pallas_call(
        last_kernel,
        in_specs=[SMEM] + [VMEM] * 5,
        out_specs=[VMEM] * 2,
        out_shape=[slab, slab],
        compiler_params=pltpu.CompilerParams(vmem_limit_bytes=32 << 20),
        cost_estimate=pl.CostEstimate(flops=1 << 21, bytes_accessed=3 << 20, transcendentals=0),
        name="last_step",
    )(scale, parts, rhs, diag, n0, n1)


def exchange(parts, axis):
    return lax.all_to_all(parts, axis, split_axis=0, concat_axis=0, tiled=True)


def on_device(fields, depart_lists, stencil_offsets, interp_weights, diag_coef, level_scale):
    tiles = depart_lists.shape[0]
    codes = coded(depart_lists, tiles)
    lists = (to_lon(codes, 1), to_lon(codes, -1), to_far(codes))
    first = jnp.concatenate([fields[32:48], fields[64:80]], axis=0)
    other = jnp.concatenate([fields[0:32], fields[48:64]], axis=0)

    def banded(block):
        return (to_lat(block, 1), block, to_lat(block, -1))

    def fetched(bands):
        to_left, to_right, far = pack(lists, bands, 16)
        return bands + (to_lon(to_right, 1), to_lon(to_left, -1), to_far(far))

    pools = fetched(banded(first))
    adv, rhs, z, cols, up, down = first_levels(
        level_scale, codes, stencil_offsets, interp_weights, diag_coef, pools
    )
    left, right = to_lon(cols, 1), to_lon(cols, -1)
    rim = lambda edge, row: jnp.concatenate([edge[:34], left[row : row + 1], right[row : row + 1], edge[36:]], axis=0)
    below = to_lat(rim(up, 0), -1)
    above = to_lat(rim(down, 63), 1)
    n0, n1, parts = level_sums(level_scale, z, rhs, diag_coef, cols, left, right, above, below)
    parts = jnp.sum(exchange(parts, "lat"), axis=0)
    parts = exchange(jnp.broadcast_to(parts[None], (lax.axis_size("lon"),) + parts.shape), "lon")
    pressure, residual = last_step(level_scale, parts, rhs, diag_coef, n0, n1)
    adv = other_levels(codes, stencil_offsets, interp_weights, fetched(banded(other)), adv)
    return (adv, pressure, residual)


def solution(mesh):
    placed = (
        P(None, "lat", "lon"),
        P("lat", "lon", None),
        P("lat", "lon"),
        P(None, "lat", "lon"),
        P("lat", "lon"),
        P(),
    )
    return jax.shard_map(
        on_device,
        mesh=mesh,
        in_specs=placed,
        out_specs=(P(None, "lat", "lon"), P(None, "lat", "lon"), P(None, "lat", "lon")),
        check_vma=False,
    )
```

```python
import functools

import jax
import jax.numpy as jnp
from jax import lax
from jax.experimental import pallas as pl
from jax.experimental.pallas import tpu as pltpu
from jax.sharding import PartitionSpec as P

ROWS = 4
LANES = 128
SPAN = 64
F32 = jnp.float32
BF16 = jnp.bfloat16


def iota(shape, dim):
    return lax.broadcasted_iota(jnp.int32, shape, dim)


def swap(block, axis, odd):
    count = lax.axis_size(axis)
    ends = [(i, i + 1) for i in range(odd, count - 1, 2)]
    if odd and axis == "lon":
        ends.append((count - 1, 0))
    return lax.ppermute(block, axis, ends + [(b, a) for a, b in ends])


def swaps(even_block, odd_block, axis):
    return swap(even_block, axis, 0), swap(odd_block, axis, 1)


def from_pole(block, ends):
    sectors = lax.axis_size("lon")
    pairs = [
        (source * sectors + s, band * sectors + (s + sectors // 2) % sectors)
        for source, band in ends
        for s in range(sectors)
    ]
    return lax.ppermute(block, ("lat", "lon"), pairs)


def from_far(block):
    last = lax.axis_size("lat") - 1
    return from_pole(block, ((0, 0), (last, last)))


def from_far_next(block):
    last = lax.axis_size("lat") - 1
    return from_pole(block, ((1, 0), (last - 1, last)))


def after(block, *others):
    return lax.optimization_barrier((block,) + others)[0]


def coded(depart_lists, tiles):
    bands, sectors = lax.axis_size("lat"), lax.axis_size("lon")
    band, sector = lax.axis_index("lat"), lax.axis_index("lon")
    wanted = depart_lists.reshape(1, -1)
    owner = wanted // tiles
    theirs = owner % sectors
    turn = jnp.where(theirs == (sector ^ 1), 1, 2)
    turn = jnp.where(theirs == (sector + sectors // 2) % sectors, 3, turn)
    turn = jnp.where(theirs == sector, 0, turn)
    source = owner // sectors
    place = jnp.where(source == band, 0, jnp.where(source == (band ^ 1), 1, 2))
    code = turn * SPAN + place * tiles + wanted % tiles
    return jnp.pad(code, ((0, 0), (0, LANES - code.shape[1])), constant_values=4 * SPAN)


def flat(rows):
    return pl.BlockSpec((rows, LANES), lambda g: (0, 0))


def ranks(member):
    before = (iota((LANES, LANES), 0) < iota((LANES, LANES), 1)).astype(BF16)
    ones = jnp.where(member, 1.0, 0.0).astype(BF16)
    return jnp.dot(ones, before, preferred_element_type=F32)


def pack_kernel(count, *refs):
    lists, (own, next_even, next_odd), outs, pick = refs[:count], refs[count : count + 3], refs[count + 3 : -1], refs[-1]

    @pl.when(pl.program_id(0) == 0)
    def _():
        sub = iota((8, LANES), 0)
        codes = jnp.where(sub == 0, lists[0][...], lists[1][...])
        if count > 2:
            far_codes = lists[2][0].astype(F32)[:8].astype(jnp.int32)
            codes = jnp.where(sub == 2, far_codes, codes)
        member = (codes >> 6) == sub + 1
        rank = jnp.where(member, ranks(member), -1.0)
        tile = ((codes & (SPAN - 1)) + 1).astype(F32)
        slot = (iota((64, LANES), 0) >> 2).astype(F32)
        row = (iota((64, 192), 0) & 3).astype(F32)
        col = iota((64, 192), 1).astype(F32)
        for d in range(count):
            hit = rank[d : d + 1] == slot
            held = jnp.sum(jnp.where(hit, tile[d : d + 1], 0.0), axis=1, keepdims=True) - 1.0
            pick[d * 64 : (d + 1) * 64, :] = jnp.where(col == held * 4.0 + row, 1.0, 0.0).astype(BF16)

    def pair(g, carry):
        pool = jnp.concatenate(
            [jnp.concatenate([ref[f] for ref in (own, next_even, next_odd)], axis=0) for f in (2 * g, 2 * g + 1)],
            axis=1,
        )
        got = jnp.dot(pick[...], pool, preferred_element_type=F32).astype(BF16)
        for d, out in enumerate(outs):
            for half in range(2):
                out[2 * g + half] = got[d * 64 : (d + 1) * 64, half * LANES : (half + 1) * LANES]
        return carry

    lax.fori_loop(0, 8, pair, 0, unroll=8)


def pack(lists, bands, blocks, of):
    levels, count = 16 * blocks, len(lists)
    source = pl.BlockSpec((16, 64, LANES), lambda g: (of(g), 0, 0))
    block = pl.BlockSpec((16, 64, LANES), lambda g: (g, 0, 0))
    rows = [flat(1)] * 2 + [pl.BlockSpec((1, 64, LANES), lambda g: (32, 0, 0))] * (count - 2)
    return pl.pallas_call(
        functools.partial(pack_kernel, count),
        grid=(blocks,),
        in_specs=rows + [source] * 3,
        out_specs=[block] * count,
        out_shape=[jax.ShapeDtypeStruct((levels, 64, LANES), BF16)] * count,
        scratch_shapes=[pltpu.VMEM((count * 64, 192), BF16)],
        compiler_params=pltpu.CompilerParams(vmem_limit_bytes=32 << 20),
        cost_estimate=pl.CostEstimate(
            flops=levels * 2 * 192 * 192 * LANES, bytes_accessed=levels * 5 * 64 * LANES * 2, transcendentals=0
        ),
        name="pack",
    )(*lists, *bands)


def set_gather(codes_ref, gather, far_slots):
    codes = jnp.broadcast_to(codes_ref[...], (8, LANES))
    turn = codes >> 6
    sub = iota((8, LANES), 0)
    rank = ranks(turn == sub)
    turn, tile = turn[:1], codes[:1] & (SPAN - 1)
    place = jnp.where(turn == 0, tile.astype(F32), -1.0)
    place = jnp.where(turn == 1, 48.0 + rank[1:2], place)
    place = jnp.where(turn == 2, 64.0 + rank[2:3], place)
    if far_slots:
        across = 80.0 + rank[3:4]
    else:
        across = ((tile & 15) + jnp.where(tile < 16, 80, 96)).astype(F32)
    place = jnp.where(turn == 3, across, place)
    row = iota((LANES, LANES), 0)
    mine = iota((LANES, LANES), 1) == 2 * (row & 15) + (row >> 6)
    place = jnp.sum(jnp.where(mine, place, 0.0), axis=1, keepdims=True)
    within = ((iota(gather.shape, 0) >> 4) & 3).astype(F32)
    col = iota(gather.shape, 1).astype(F32)
    gather[...] = jnp.where(col == place * 4.0 + within, 1.0, 0.0).astype(BF16)


def every_fourth(q):
    return pl.ds(q, 16, stride=4)


def set_weights(offsets, weights, coef):
    for q in range(4):
        offset = offsets[every_fourth(q), :]
        points = [weights[m, every_fourth(q), :] for m in range(4)]
        for r in range(8):
            value = jnp.zeros((16, LANES), F32)
            for m in range(4):
                if 0 <= r - m <= 4:
                    value = jnp.where(offset == r - m, points[m], value)
            coef[q * 8 + r] = value


def interpolate(gather, coef, first_pools, second_pools, first, second=None):
    second = first if second is None else second
    pool = jnp.concatenate(
        [
            jnp.concatenate([ref[f] for ref in pools], axis=0)
            for pools, f in ((first_pools, first), (second_pools, second))
        ],
        axis=1,
    )
    rows = jnp.dot(gather[...], pool, preferred_element_type=F32)
    out = []
    for q in range(4):
        sums = [None, None]
        for r in range(8):
            weight = coef[q * 8 + r]
            for h in range(2):
                term = weight * rows[r * 16 : (r + 1) * 16, h * LANES : (h + 1) * LANES]
                sums[h] = term if r == 0 else sums[h] + term
        out.append(sums)
    return out


def levels_block(of):
    return pl.BlockSpec((16, 64, LANES), lambda g: (of(g), 0, 0))


SMEM = pl.BlockSpec(memory_space=pltpu.SMEM)
VMEM = pl.BlockSpec(memory_space=pltpu.VMEM)
WEIGHTS = pl.BlockSpec((4, 64, LANES), lambda g: (0, 0, 0))


def scratch(pool):
    return [
        pltpu.VMEM((LANES, 64 * pool), BF16), pltpu.VMEM((32, 16, LANES), F32), pltpu.VMEM((16, 64, LANES), F32)
    ]


def first_kernel(scale, codes, offsets, weights, diag, *refs):
    middle, top = refs[0:7], refs[7:14]
    adv, rhs, cols, edge_even, edge_odd, own_up, own_down, gather, coef, tmp = refs[14:]
    set_gather(codes, gather, False)
    set_weights(offsets, weights, coef)

    def level(l, carry):
        values = interpolate(gather, coef, middle, top, l)
        for q in range(4):
            tmp[l, every_fourth(q), :] = values[q][0]
            rhs[l, every_fourth(q), :] = values[q][1] + 0.5 * values[q][0]
        return carry

    lax.fori_loop(0, 16, level, 0, unroll=8)
    group = iota((64, LANES), 1) >> 2
    packed = jnp.where(group == 16, pltpu.roll(diag[...], 65, 1), 0.0)
    for l in range(16):
        adv[l] = tmp[l].astype(BF16)
        value = rhs[l] / (4.0 + diag[...] * scale[l])
        for ref, ends in ((own_up, (0, 1)), (own_down, (63, 62))):
            for place, r in enumerate(ends):
                ref[16 * place + l : 16 * place + l + 1, :] = value[r : r + 1]
        packed = jnp.where(group == l, pltpu.roll(value, 2 + 4 * l, 1), packed)
    cols[...] = packed
    for ref, r in ((own_up, 0), (own_down, 63)):
        ref[32:33, :] = diag[r : r + 1, :]
        ref[33:40, :] = jnp.ones((7, LANES), F32)
    up, down = own_up[...], own_down[...]
    even_band = lax.rem(lax.axis_index("lat"), 2) == 0
    edge_even[...] = jnp.where(even_band, down, up)
    edge_odd[...] = jnp.where(even_band, up, down)


def first_levels(scale, codes, offsets, weights, diag, bands, slots, far):
    slab = jax.ShapeDtypeStruct((16, 64, LANES), F32)
    edge = jax.ShapeDtypeStruct((40, LANES), F32)
    whole = levels_block(lambda g: 0)
    pools, specs = [], []
    for half in range(2):
        pools += [*bands, *slots, *far]
        specs += [levels_block(lambda g, half=half: 2 + 2 * half)] * 3 + [levels_block(lambda g, half=half: half)] * 4
    return pl.pallas_call(
        first_kernel,
        grid=(1,),
        in_specs=[SMEM, flat(1), flat(64), WEIGHTS, flat(64)] + specs,
        out_specs=[levels_block(lambda g: 2), whole, flat(64)] + [flat(40)] * 4,
        out_shape=[
            jax.ShapeDtypeStruct((64, 64, LANES), BF16), slab, jax.ShapeDtypeStruct((64, LANES), F32)
        ] + [edge] * 4,
        scratch_shapes=scratch(7),
        compiler_params=pltpu.CompilerParams(vmem_limit_bytes=60 << 20),
        cost_estimate=pl.CostEstimate(flops=32 * 2 * 128 * 448 * 128, bytes_accessed=6 << 20, transcendentals=0),
        name="first_levels",
    )(scale, codes, offsets, weights, diag, *pools)


def other_kernel(codes, offsets, weights, *refs):
    pools, (start, adv, gather, coef, tmp) = refs[:6], refs[6:]

    @pl.when(pl.program_id(0) == 0)
    def _():
        set_gather(codes, gather, True)
        set_weights(offsets, weights, coef)

    def pair(g, carry):
        values = interpolate(gather, coef, pools, pools, 2 * g, 2 * g + 1)
        for h in range(2):
            for q in range(4):
                tmp[2 * g + h, every_fourth(q), :] = values[q][h]
        return carry

    lax.fori_loop(0, 8, pair, 0, unroll=8)
    for f in range(16):
        adv[f] = tmp[f].astype(BF16)


def other_levels(codes, offsets, weights, bands, slots, start):
    return pl.pallas_call(
        other_kernel,
        grid=(3,),
        in_specs=[flat(1), flat(64), WEIGHTS]
        + [levels_block(lambda g: g + g // 2)] * 3
        + [levels_block(lambda g: g)] * 3
        + [pl.BlockSpec(memory_space=pl.ANY)],
        out_specs=levels_block(lambda g: g + g // 2),
        out_shape=jax.ShapeDtypeStruct(start.shape, start.dtype),
        scratch_shapes=scratch(6),
        input_output_aliases={9: 0},
        compiler_params=pltpu.CompilerParams(vmem_limit_bytes=32 << 20),
        cost_estimate=pl.CostEstimate(flops=48 * 2 * 128 * 448 * 128, bytes_accessed=6 << 20, transcendentals=0),
        name="other_levels",
    )(codes, offsets, weights, *bands, *slots, start)


def sum_kernel(scale, rhs, diag, cols, own_up, own_down, cols_even, cols_odd, edge_even, edge_odd, n0, n1, sums, rowsums):
    lane = iota((64, LANES), 1)
    even_band = lax.rem(lax.axis_index("lat"), 2) == 0
    even_sector = lax.rem(lax.axis_index("lon"), 2) == 0
    even, odd = edge_even[...], edge_odd[...]
    above, below = jnp.where(even_band, odd, even), jnp.where(even_band, even, odd)
    even, odd = cols_even[...], cols_odd[...]
    left, right = jnp.where(even_sector, odd, even), jnp.where(even_sector, even, odd)
    spread = jnp.zeros((1, LANES), F32)
    column = jnp.zeros((16, LANES), F32)
    for l in range(16):
        spread = jnp.where((lane[:1] >> 2) == l, scale[l], spread)
        column = jnp.where(iota((16, LANES), 0) == l, scale[l], column)
    row16, lane16 = iota((16, LANES), 0), lane[:16]

    west_even, west_odd = left[64:80, LANES - 1 : LANES], left[80:96, LANES - 1 : LANES]
    east_even, east_odd = right[64:80, 0:1], right[80:96, 0:1]
    corners = [
        [jnp.where(even_band, west_odd, west_even), jnp.where(even_band, east_odd, east_even)],
        [jnp.where(even_band, west_even, west_odd), jnp.where(even_band, east_even, east_odd)],
    ]

    def spread_corner(column, which):
        return jnp.sum(jnp.where(lane16 == 4 * row16 + which, column, 0.0), axis=0, keepdims=True)

    def rim_row(edge, inner, west, east):
        near, second, flag = edge[0:16, :], edge[16:32, :], edge[33:34, :]
        beside = jnp.where(lane16 == 0, west, pltpu.roll(near, 1, 1))
        beside = beside + jnp.where(lane16 == LANES - 1, east, pltpu.roll(near, LANES - 1, 1))
        return flag * (second + inner + beside) / (4.0 + edge[32:33, :] * column)

    top, bottom = rim_row(above, own_up[0:16, :], *corners[0]), rim_row(below, own_down[0:16, :], *corners[1])

    def rim_col(edge, side, which, toward, diag_lane):
        values = edge[0:64]
        first, last = (spread_corner(pair[side], which) for pair in corners)
        up = jnp.concatenate([first, values[:-1]], axis=0)
        down = jnp.concatenate([values[1:], last], axis=0)
        outer = pltpu.roll(values, toward % LANES, 1)
        inner = pltpu.roll(cols[...], -toward % LANES, 1)
        coef = 4.0 + values[:, diag_lane : diag_lane + 1] * spread
        return (up + down + outer + inner) / coef

    west = rim_col(left, 0, 1, 1, 64)
    east = rim_col(right, 1, 2, -1, 65)

    def beside(value, west_col, east_col, upper, lower):
        total = jnp.where(lane == 0, west_col, pltpu.roll(value, 1, 1))
        total = total + jnp.where(lane == LANES - 1, east_col, pltpu.roll(value, LANES - 1, 1))
        total = total + jnp.concatenate([upper, value[:-1]], axis=0)
        return total + jnp.concatenate([value[1:], lower], axis=0)

    for l in range(16):
        start = rhs[l]
        inverse = 1.0 / (4.0 + diag[...] * scale[l])
        value = start * inverse
        around = beside(
            value, left[0:64, 4 * l + 1 : 4 * l + 2], right[0:64, 4 * l + 2 : 4 * l + 3], above[l : l + 1, :], below[l : l + 1, :]
        )
        n0[l] = around
        again = around * inverse
        second = beside(
            again, west[:, 4 * l + 1 : 4 * l + 2], east[:, 4 * l + 2 : 4 * l + 3], top[l : l + 1], bottom[l : l + 1]
        )
        n1[l] = second
        for k, term in enumerate((start * value, start * again, around * again, second * again)):
            part = term[0:8]
            for j in range(1, 8):
                part = part + term[8 * j : 8 * j + 8]
            rowsums[k * 16 + l : k * 16 + l + 1, :] = jnp.sum(part, axis=0, keepdims=True)
    total = jnp.sum(rowsums[...], axis=1, keepdims=True)
    packed = jnp.zeros((8, LANES), F32)
    for j in range(8):
        packed = jnp.where(lane[:8] == j, total[8 * j : 8 * j + 8], packed)
    for j in range(sums.shape[0]):
        sums[j] = packed


def level_sums(scale, rhs, diag, cols, own, cols_rim, edges):
    slab = jax.ShapeDtypeStruct((16, 64, LANES), F32)
    return pl.pallas_call(
        sum_kernel,
        in_specs=[SMEM] + [VMEM] * 9,
        out_specs=[VMEM] * 3,
        out_shape=[slab, slab, jax.ShapeDtypeStruct((lax.axis_size("lat"), 8, LANES), F32)],
        scratch_shapes=[pltpu.VMEM((64, LANES), F32)],
        compiler_params=pltpu.CompilerParams(vmem_limit_bytes=60 << 20),
        cost_estimate=pl.CostEstimate(flops=1 << 22, bytes_accessed=2 << 20, transcendentals=0),
        name="level_sums",
    )(scale, rhs, diag, cols, *own, *cols_rim, *edges)


def last_kernel(scale, parts, rhs, diag, n0, n1, pressure, residual):
    total = parts[0]
    for j in range(1, parts.shape[0]):
        total = total + parts[j]
    lane = iota((8, LANES), 1)

    def of(k, half):
        return jnp.sum(jnp.where(lane == 2 * k + half, total, 0.0), axis=1, keepdims=True)

    for half in range(2):
        s0, s1, s2, s3 = (of(k, half) for k in range(4))
        curve = s0 - s1
        step = s0 / curve
        keep = -s1 / curve
        norm = keep * keep * s0 + 2.0 * keep * step * s1 + step * step * s2
        ratio = norm / s0
        bend = norm - (keep * keep * s1 + 2.0 * keep * step * s2 + step * step * s3)
        other = norm / (bend - ratio * ratio * curve)
        along = other * (keep + ratio)
        across = other * step
        fit_z, fit_p = step + along, across
        fit_r, fit_n0, fit_n1 = keep - along, step + along - across, across
        for s in range(8):
            l = 8 * half + s
            at = lambda column: column[s : s + 1]
            inverse = 1.0 / (4.0 + diag[...] * scale[l])
            start, around = rhs[l], n0[l]
            pressure[l] = (at(fit_z) * start + at(fit_p) * around) * inverse
            residual[l] = at(fit_r) * start + at(fit_n0) * around + at(fit_n1) * n1[l]


def last_step(scale, parts, rhs, diag, n0, n1):
    slab = jax.ShapeDtypeStruct((16, 64, LANES), F32)
    return pl.pallas_call(
        last_kernel,
        in_specs=[SMEM] + [VMEM] * 5,
        out_specs=[VMEM] * 2,
        out_shape=[slab, slab],
        compiler_params=pltpu.CompilerParams(vmem_limit_bytes=60 << 20),
        cost_estimate=pl.CostEstimate(flops=1 << 21, bytes_accessed=3 << 20, transcendentals=0),
        name="last_step",
    )(scale, parts, rhs, diag, n0, n1)


def exchange(parts, axis):
    return lax.all_to_all(parts, axis, split_axis=0, concat_axis=0, tiled=True)


def on_device(fields, depart_lists, stencil_offsets, interp_weights, diag_coef, level_scale):
    tiles = depart_lists.shape[0]
    codes = coded(depart_lists, tiles)
    bands = (fields,) + swaps(fields, fields, "lat")
    lists = swaps(codes, codes, "lon")
    rows = jnp.broadcast_to(codes.astype(BF16)[None], (1, 64, LANES))
    first = after(jnp.concatenate([fields[32:48], fields[64:80], rows], axis=0), *lists)
    first_far = (from_far(first), from_far_next(first))
    first_out = pack(lists, bands, 2, lambda g: 2 + 2 * g)
    first_slots = swaps(*first_out, "lon")
    later = after(lists[0], *first_out, *first_far)
    *other_out, other_far = pack((later, lists[1], first_far[0]), bands, 3, lambda g: g + g // 2)
    other_slots = swaps(*other_out, "lon")
    first_slots = (after(first_slots[0], *other_out), first_slots[1])
    adv, rhs, cols, *edges = first_levels(
        level_scale, codes, stencil_offsets, interp_weights, diag_coef, bands, first_slots, first_far
    )
    own, edges = edges[2:], swaps(*edges[:2], "lat")
    rim = jnp.concatenate([cols, edges[0][:16], edges[1][:16]], axis=0)
    cols_rim = swaps(rim, rim, "lon")
    other_far = from_far(after(other_far, *cols_rim))
    n0, n1, parts = level_sums(level_scale, rhs, diag_coef, cols, own, cols_rim, edges)
    parts = jnp.sum(exchange(parts, "lat"), axis=0)
    parts = exchange(jnp.broadcast_to(parts[None], (lax.axis_size("lon"),) + parts.shape), "lon")
    adv = other_levels(codes, stencil_offsets, interp_weights, bands, other_slots + (other_far,), adv)
    parts = after(parts, adv)
    pressure, residual = last_step(level_scale, parts, rhs, diag_coef, n0, n1)
    return (adv, pressure, residual)


def solution(mesh):
    placed = (
        P(None, "lat", "lon"),
        P("lat", "lon", None),
        P("lat", "lon"),
        P(None, "lat", "lon"),
        P("lat", "lon"),
        P(),
    )
    return jax.shard_map(
        on_device,
        mesh=mesh,
        in_specs=placed,
        out_specs=(P(None, "lat", "lon"), P(None, "lat", "lon"), P(None, "lat", "lon")),
        check_vma=False,
    )
```

```python
import functools

import jax
import jax.numpy as jnp
from jax import lax
from jax.experimental import pallas as pl
from jax.experimental.pallas import tpu as pltpu
from jax.sharding import PartitionSpec as P

ROWS = 4
LANES = 128
SPAN = 64
F32 = jnp.float32
BF16 = jnp.bfloat16


def iota(shape, dim):
    return lax.broadcasted_iota(jnp.int32, shape, dim)


def swap(block, axis, odd):
    count = lax.axis_size(axis)
    ends = [(i, i + 1) for i in range(odd, count - 1, 2)]
    if odd and axis == "lon":
        ends.append((count - 1, 0))
    return lax.ppermute(block, axis, ends + [(b, a) for a, b in ends])


def swaps(even_block, odd_block, axis):
    return swap(even_block, axis, 0), swap(odd_block, axis, 1)


def from_pole(block, ends):
    sectors = lax.axis_size("lon")
    pairs = [
        (source * sectors + s, band * sectors + (s + sectors // 2) % sectors)
        for source, band in ends
        for s in range(sectors)
    ]
    return lax.ppermute(block, ("lat", "lon"), pairs)


def from_far(block):
    last = lax.axis_size("lat") - 1
    return from_pole(block, ((0, 0), (last, last)))


def from_far_next(block):
    last = lax.axis_size("lat") - 1
    return from_pole(block, ((1, 0), (last - 1, last)))


def after(block, *others):
    return lax.optimization_barrier((block,) + others)[0]


def coded(depart_lists, tiles):
    bands, sectors = lax.axis_size("lat"), lax.axis_size("lon")
    band, sector = lax.axis_index("lat"), lax.axis_index("lon")
    wanted = depart_lists.transpose(1, 2, 0).reshape(1, -1)
    owner = wanted // tiles
    theirs = owner % sectors
    turn = jnp.where(theirs == (sector ^ 1), 1, 2)
    turn = jnp.where(theirs == (sector + sectors // 2) % sectors, 3, turn)
    turn = jnp.where(theirs == sector, 0, turn)
    source = owner // sectors
    place = jnp.where(source == band, 0, jnp.where(source == (band ^ 1), 1, 2))
    code = turn * SPAN + place * tiles + wanted % tiles
    return jnp.pad(code, ((0, 0), (0, LANES - code.shape[1])), constant_values=4 * SPAN)


def flat(rows):
    return pl.BlockSpec((rows, LANES), lambda g: (0, 0))


def ranks(member):
    before = (iota((LANES, LANES), 0) < iota((LANES, LANES), 1)).astype(BF16)
    ones = jnp.where(member, 1.0, 0.0).astype(BF16)
    return jnp.dot(ones, before, preferred_element_type=F32)


def pack_kernel(count, *refs):
    lists, (own, next_even, next_odd), outs, pick = refs[:count], refs[count : count + 3], refs[count + 3 : -1], refs[-1]

    @pl.when(pl.program_id(0) == 0)
    def _():
        sub = iota((8, LANES), 0)
        codes = jnp.where(sub == 0, lists[0][...], lists[1][...])
        if count > 2:
            far_codes = lists[2][0].astype(F32)[:8].astype(jnp.int32)
            codes = jnp.where(sub == 2, far_codes, codes)
        member = (codes >> 6) == sub + 1
        rank = jnp.where(member, ranks(member), -1.0)
        tile = ((codes & (SPAN - 1)) + 1).astype(F32)
        slot = (iota((64, LANES), 0) >> 2).astype(F32)
        row = (iota((64, 192), 0) & 3).astype(F32)
        col = iota((64, 192), 1).astype(F32)
        for d in range(count):
            hit = rank[d : d + 1] == slot
            held = jnp.sum(jnp.where(hit, tile[d : d + 1], 0.0), axis=1, keepdims=True) - 1.0
            pick[d * 64 : (d + 1) * 64, :] = jnp.where(col == held * 4.0 + row, 1.0, 0.0).astype(BF16)

    def pair(g, carry):
        pool = jnp.concatenate(
            [jnp.concatenate([ref[f] for ref in (own, next_even, next_odd)], axis=0) for f in (2 * g, 2 * g + 1)],
            axis=1,
        )
        got = jnp.dot(pick[...], pool, preferred_element_type=F32).astype(BF16)
        for d, out in enumerate(outs):
            for half in range(2):
                out[2 * g + half] = got[d * 64 : (d + 1) * 64, half * LANES : (half + 1) * LANES]
        return carry

    lax.fori_loop(0, 8, pair, 0, unroll=8)


def pack(lists, bands, blocks, of):
    levels, count = 16 * blocks, len(lists)
    source = pl.BlockSpec((16, 64, LANES), lambda g: (of(g), 0, 0))
    block = pl.BlockSpec((16, 64, LANES), lambda g: (g, 0, 0))
    rows = [flat(1)] * 2 + [pl.BlockSpec((1, 64, LANES), lambda g: (32, 0, 0))] * (count - 2)
    return pl.pallas_call(
        functools.partial(pack_kernel, count),
        grid=(blocks,),
        in_specs=rows + [source] * 3,
        out_specs=[block] * count,
        out_shape=[jax.ShapeDtypeStruct((levels, 64, LANES), BF16)] * count,
        scratch_shapes=[pltpu.VMEM((count * 64, 192), BF16)],
        compiler_params=pltpu.CompilerParams(vmem_limit_bytes=32 << 20),
        cost_estimate=pl.CostEstimate(
            flops=levels * 2 * 192 * 192 * LANES, bytes_accessed=levels * 5 * 64 * LANES * 2, transcendentals=0
        ),
        name="pack",
    )(*lists, *bands)


def set_gather(codes_ref, gather, far_slots):
    codes = jnp.broadcast_to(codes_ref[...], (8, LANES))
    turn = codes >> 6
    sub = iota((8, LANES), 0)
    rank = ranks(turn == sub)
    turn, tile = turn[:1], codes[:1] & (SPAN - 1)
    place = jnp.where(turn == 0, tile.astype(F32), -1.0)
    place = jnp.where(turn == 1, 48.0 + rank[1:2], place)
    place = jnp.where(turn == 2, 64.0 + rank[2:3], place)
    if far_slots:
        across = 80.0 + rank[3:4]
    else:
        across = ((tile & 15) + jnp.where(tile < 16, 80, 96)).astype(F32)
    place = jnp.where(turn == 3, across, place)
    row = iota((LANES, LANES), 0)
    mine = iota((LANES, LANES), 1) == (row & 15) + 16 * (row >> 6)
    place = jnp.sum(jnp.where(mine, place, 0.0), axis=1, keepdims=True)
    within = ((iota(gather.shape, 0) >> 4) & 3).astype(F32)
    col = iota(gather.shape, 1).astype(F32)
    gather[...] = jnp.where(col == place * 4.0 + within, 1.0, 0.0).astype(BF16)


def every_fourth(q):
    return pl.ds(q, 16, stride=4)


def set_weights(offsets, weights, coef):
    for q in range(4):
        offset = offsets[every_fourth(q), :]
        points = [weights[m, every_fourth(q), :] for m in range(4)]
        for r in range(8):
            value = jnp.zeros((16, LANES), F32)
            for m in range(4):
                if 0 <= r - m <= 4:
                    value = jnp.where(offset == r - m, points[m], value)
            coef[q * 8 + r] = value


def interpolate(gather, coef, first_pools, second_pools, first, second=None):
    second = first if second is None else second
    pool = jnp.concatenate(
        [
            jnp.concatenate([ref[f] for ref in pools], axis=0)
            for pools, f in ((first_pools, first), (second_pools, second))
        ],
        axis=1,
    )
    rows = jnp.dot(gather[...], pool, preferred_element_type=F32)
    out = []
    for q in range(4):
        sums = [None, None]
        for r in range(8):
            weight = coef[q * 8 + r]
            for h in range(2):
                term = weight * rows[r * 16 : (r + 1) * 16, h * LANES : (h + 1) * LANES]
                sums[h] = term if r == 0 else sums[h] + term
        out.append(sums)
    return out


def levels_block(of):
    return pl.BlockSpec((16, 64, LANES), lambda g: (of(g), 0, 0))


SMEM = pl.BlockSpec(memory_space=pltpu.SMEM)
VMEM = pl.BlockSpec(memory_space=pltpu.VMEM)
WEIGHTS = pl.BlockSpec((4, 64, LANES), lambda g: (0, 0, 0))


def scratch(pool):
    return [
        pltpu.VMEM((LANES, 64 * pool), BF16), pltpu.VMEM((32, 16, LANES), F32), pltpu.VMEM((16, 64, LANES), F32)
    ]


def first_kernel(scale, codes, offsets, weights, diag, *refs):
    middle, top = refs[0:7], refs[7:14]
    adv, rhs, cols, edge_even, edge_odd, own_up, own_down, gather, coef, tmp = refs[14:]
    set_gather(codes, gather, False)
    set_weights(offsets, weights, coef)

    def level(l, carry):
        values = interpolate(gather, coef, middle, top, l)
        for q in range(4):
            tmp[l, every_fourth(q), :] = values[q][0]
            rhs[l, every_fourth(q), :] = values[q][1] + 0.5 * values[q][0]
        return carry

    lax.fori_loop(0, 16, level, 0, unroll=16)
    group = iota((64, LANES), 1) >> 2
    packed = jnp.where(group == 16, pltpu.roll(diag[...], 65, 1), 0.0)
    for l in range(16):
        adv[l] = tmp[l].astype(BF16)
        value = rhs[l] / (4.0 + diag[...] * scale[l])
        for ref, ends in ((own_up, (0, 1)), (own_down, (63, 62))):
            for place, r in enumerate(ends):
                ref[16 * place + l : 16 * place + l + 1, :] = value[r : r + 1]
        packed = jnp.where(group == l, pltpu.roll(value, 2 + 4 * l, 1), packed)
    cols[...] = packed
    for ref, r in ((own_up, 0), (own_down, 63)):
        ref[32:33, :] = diag[r : r + 1, :]
        ref[33:40, :] = jnp.ones((7, LANES), F32)
    up, down = own_up[...], own_down[...]
    even_band = lax.rem(lax.axis_index("lat"), 2) == 0
    edge_even[...] = jnp.where(even_band, down, up)
    edge_odd[...] = jnp.where(even_band, up, down)


def first_levels(scale, codes, offsets, weights, diag, bands, slots, far):
    slab = jax.ShapeDtypeStruct((16, 64, LANES), F32)
    edge = jax.ShapeDtypeStruct((40, LANES), F32)
    whole = levels_block(lambda g: 0)
    pools, specs = [], []
    for half in range(2):
        pools += [*bands, *slots, *far]
        specs += [levels_block(lambda g, half=half: 2 + 2 * half)] * 3 + [levels_block(lambda g, half=half: half)] * 4
    return pl.pallas_call(
        first_kernel,
        grid=(1,),
        in_specs=[SMEM, flat(1), flat(64), WEIGHTS, flat(64)] + specs,
        out_specs=[levels_block(lambda g: 2), whole, flat(64)] + [flat(40)] * 4,
        out_shape=[
            jax.ShapeDtypeStruct((64, 64, LANES), BF16), slab, jax.ShapeDtypeStruct((64, LANES), F32)
        ] + [edge] * 4,
        scratch_shapes=scratch(7),
        compiler_params=pltpu.CompilerParams(vmem_limit_bytes=32 << 20),
        cost_estimate=pl.CostEstimate(flops=32 * 2 * 128 * 448 * 128, bytes_accessed=6 << 20, transcendentals=0),
        name="first_levels",
    )(scale, codes, offsets, weights, diag, *pools)


def other_kernel(codes, offsets, weights, *refs):
    pools, (start, adv, gather, coef, tmp) = refs[:6], refs[6:]

    @pl.when(pl.program_id(0) == 0)
    def _():
        set_gather(codes, gather, True)
        set_weights(offsets, weights, coef)

    def pair(g, carry):
        values = interpolate(gather, coef, pools, pools, 2 * g, 2 * g + 1)
        for h in range(2):
            for q in range(4):
                tmp[2 * g + h, every_fourth(q), :] = values[q][h]
        return carry

    lax.fori_loop(0, 8, pair, 0, unroll=8)
    for f in range(16):
        adv[f] = tmp[f].astype(BF16)


def other_levels(codes, offsets, weights, bands, slots, start):
    return pl.pallas_call(
        other_kernel,
        grid=(3,),
        in_specs=[flat(1), flat(64), WEIGHTS]
        + [levels_block(lambda g: g + g // 2)] * 3
        + [levels_block(lambda g: g)] * 3
        + [pl.BlockSpec(memory_space=pl.ANY)],
        out_specs=levels_block(lambda g: g + g // 2),
        out_shape=jax.ShapeDtypeStruct(start.shape, start.dtype),
        scratch_shapes=scratch(6),
        input_output_aliases={9: 0},
        compiler_params=pltpu.CompilerParams(vmem_limit_bytes=32 << 20),
        cost_estimate=pl.CostEstimate(flops=48 * 2 * 128 * 448 * 128, bytes_accessed=6 << 20, transcendentals=0),
        name="other_levels",
    )(codes, offsets, weights, *bands, *slots, start)


def sum_kernel(scale, rhs, diag, cols, own_up, own_down, cols_even, cols_odd, edge_even, edge_odd, n0, n1, sums, rowsums):
    lane = iota((64, LANES), 1)
    even_band = lax.rem(lax.axis_index("lat"), 2) == 0
    even_sector = lax.rem(lax.axis_index("lon"), 2) == 0
    even, odd = edge_even[...], edge_odd[...]
    above, below = jnp.where(even_band, odd, even), jnp.where(even_band, even, odd)
    even, odd = cols_even[...], cols_odd[...]
    left, right = jnp.where(even_sector, odd, even), jnp.where(even_sector, even, odd)
    spread = jnp.zeros((1, LANES), F32)
    column = jnp.zeros((16, LANES), F32)
    for l in range(16):
        spread = jnp.where((lane[:1] >> 2) == l, scale[l], spread)
        column = jnp.where(iota((16, LANES), 0) == l, scale[l], column)
    row16, lane16 = iota((16, LANES), 0), lane[:16]

    west_even, west_odd = left[64:80, LANES - 1 : LANES], left[80:96, LANES - 1 : LANES]
    east_even, east_odd = right[64:80, 0:1], right[80:96, 0:1]
    corners = [
        [jnp.where(even_band, west_odd, west_even), jnp.where(even_band, east_odd, east_even)],
        [jnp.where(even_band, west_even, west_odd), jnp.where(even_band, east_even, east_odd)],
    ]

    def spread_corner(column, which):
        return jnp.sum(jnp.where(lane16 == 4 * row16 + which, column, 0.0), axis=0, keepdims=True)

    def rim_row(edge, inner, west, east):
        near, second, flag = edge[0:16, :], edge[16:32, :], edge[33:34, :]
        beside = jnp.where(lane16 == 0, west, pltpu.roll(near, 1, 1))
        beside = beside + jnp.where(lane16 == LANES - 1, east, pltpu.roll(near, LANES - 1, 1))
        return flag * (second + inner + beside) / (4.0 + edge[32:33, :] * column)

    top, bottom = rim_row(above, own_up[0:16, :], *corners[0]), rim_row(below, own_down[0:16, :], *corners[1])

    def rim_col(edge, side, which, toward, diag_lane):
        values = edge[0:64]
        first, last = (spread_corner(pair[side], which) for pair in corners)
        up = jnp.concatenate([first, values[:-1]], axis=0)
        down = jnp.concatenate([values[1:], last], axis=0)
        outer = pltpu.roll(values, toward % LANES, 1)
        inner = pltpu.roll(cols[...], -toward % LANES, 1)
        coef = 4.0 + values[:, diag_lane : diag_lane + 1] * spread
        return (up + down + outer + inner) / coef

    west = rim_col(left, 0, 1, 1, 64)
    east = rim_col(right, 1, 2, -1, 65)

    def beside(value, west_col, east_col, upper, lower):
        total = jnp.where(lane == 0, west_col, pltpu.roll(value, 1, 1))
        total = total + jnp.where(lane == LANES - 1, east_col, pltpu.roll(value, LANES - 1, 1))
        total = total + jnp.concatenate([upper, value[:-1]], axis=0)
        return total + jnp.concatenate([value[1:], lower], axis=0)

    for l in range(16):
        start = rhs[l]
        inverse = 1.0 / (4.0 + diag[...] * scale[l])
        value = start * inverse
        around = beside(
            value, left[0:64, 4 * l + 1 : 4 * l + 2], right[0:64, 4 * l + 2 : 4 * l + 3], above[l : l + 1, :], below[l : l + 1, :]
        )
        n0[l] = around
        again = around * inverse
        second = beside(
            again, west[:, 4 * l + 1 : 4 * l + 2], east[:, 4 * l + 2 : 4 * l + 3], top[l : l + 1], bottom[l : l + 1]
        )
        n1[l] = second
        for k, term in enumerate((start * value, start * again, around * again, second * again)):
            part = term[0:8]
            for j in range(1, 8):
                part = part + term[8 * j : 8 * j + 8]
            rowsums[k * 16 + l : k * 16 + l + 1, :] = jnp.sum(part, axis=0, keepdims=True)
    total = jnp.sum(rowsums[...], axis=1, keepdims=True)
    packed = jnp.sum(jnp.where(lane == iota((64, LANES), 0), total, 0.0), axis=0, keepdims=True)
    for j in range(sums.shape[0]):
        sums[j] = packed


def level_sums(scale, rhs, diag, cols, own, cols_rim, edges):
    slab = jax.ShapeDtypeStruct((16, 64, LANES), F32)
    return pl.pallas_call(
        sum_kernel,
        in_specs=[SMEM] + [VMEM] * 9,
        out_specs=[VMEM] * 3,
        out_shape=[slab, slab, jax.ShapeDtypeStruct((lax.axis_size("lat"), 1, LANES), F32)],
        scratch_shapes=[pltpu.VMEM((64, LANES), F32)],
        compiler_params=pltpu.CompilerParams(vmem_limit_bytes=60 << 20),
        cost_estimate=pl.CostEstimate(flops=1 << 22, bytes_accessed=2 << 20, transcendentals=0),
        name="level_sums",
    )(scale, rhs, diag, cols, *own, *cols_rim, *edges)


def last_kernel(scale, parts, rhs, diag, n0, n1, pressure, residual):
    total = parts[0]
    for j in range(1, parts.shape[0]):
        total = total + parts[j]
    total = jnp.broadcast_to(total, (8, LANES))
    lane, row = iota((8, LANES), 1), iota((8, LANES), 0)

    def of(k, half):
        return jnp.sum(jnp.where(lane == 16 * k + 8 * half + row, total, 0.0), axis=1, keepdims=True)

    for half in range(2):
        s0, s1, s2, s3 = (of(k, half) for k in range(4))
        curve = s0 - s1
        step = s0 / curve
        keep = -s1 / curve
        norm = keep * keep * s0 + 2.0 * keep * step * s1 + step * step * s2
        ratio = norm / s0
        bend = norm - (keep * keep * s1 + 2.0 * keep * step * s2 + step * step * s3)
        other = norm / (bend - ratio * ratio * curve)
        along = other * (keep + ratio)
        across = other * step
        fit_z, fit_p = step + along, across
        fit_r, fit_n0, fit_n1 = keep - along, step + along - across, across
        for s in range(8):
            l = 8 * half + s
            at = lambda column: column[s : s + 1]
            inverse = 1.0 / (4.0 + diag[...] * scale[l])
            start, around = rhs[l], n0[l]
            pressure[l] = (at(fit_z) * start + at(fit_p) * around) * inverse
            residual[l] = at(fit_r) * start + at(fit_n0) * around + at(fit_n1) * n1[l]


def last_step(scale, parts, rhs, diag, n0, n1):
    slab = jax.ShapeDtypeStruct((16, 64, LANES), F32)
    return pl.pallas_call(
        last_kernel,
        in_specs=[SMEM] + [VMEM] * 5,
        out_specs=[VMEM] * 2,
        out_shape=[slab, slab],
        input_output_aliases={2: 1, 4: 0},
        compiler_params=pltpu.CompilerParams(vmem_limit_bytes=60 << 20),
        cost_estimate=pl.CostEstimate(flops=1 << 21, bytes_accessed=3 << 20, transcendentals=0),
        name="last_step",
    )(scale, parts, rhs, diag, n0, n1)


def exchange(parts, axis):
    return lax.all_to_all(parts, axis, split_axis=0, concat_axis=0, tiled=True)


def on_device(fields, depart_lists, stencil_offsets, interp_weights, diag_coef, level_scale):
    tiles = depart_lists.shape[0]
    codes = coded(depart_lists, tiles)
    bands = (fields,) + swaps(fields, fields, "lat")
    lists = swaps(codes, codes, "lon")
    rows = jnp.broadcast_to(codes.astype(BF16)[None], (1, 64, LANES))
    first = after(jnp.concatenate([fields[32:48], fields[64:80], rows], axis=0), *lists)
    first_far = (from_far(first), from_far_next(first))
    first_out = pack(lists, bands, 2, lambda g: 2 + 2 * g)
    first_slots = swaps(*first_out, "lon")
    later = after(lists[0], *first_out, *first_far)
    *other_out, other_far = pack((later, lists[1], first_far[0]), bands, 3, lambda g: g + g // 2)
    other_slots = swaps(*other_out, "lon")
    first_slots = (after(first_slots[0], *other_out), first_slots[1])
    adv, rhs, cols, *edges = first_levels(
        level_scale, codes, stencil_offsets, interp_weights, diag_coef, bands, first_slots, first_far
    )
    own, edges = edges[2:], swaps(*edges[:2], "lat")
    rim = jnp.concatenate([cols, edges[0][:16], edges[1][:16]], axis=0)
    cols_rim = swaps(rim, rim, "lon")
    other_far = from_far(after(other_far, *cols_rim))
    n0, n1, parts = level_sums(level_scale, rhs, diag_coef, cols, own, cols_rim, edges)
    parts = jnp.sum(exchange(parts, "lat"), axis=0)
    parts = exchange(jnp.broadcast_to(parts[None], (lax.axis_size("lon"),) + parts.shape), "lon")
    adv = other_levels(codes, stencil_offsets, interp_weights, bands, other_slots + (other_far,), adv)
    parts = after(parts, adv)
    pressure, residual = last_step(level_scale, parts, rhs, diag_coef, n0, n1)
    return (adv, pressure, residual)


def solution(mesh):
    placed = (
        P(None, "lat", "lon"),
        P("lat", "lon", None),
        P("lat", "lon"),
        P(None, "lat", "lon"),
        P("lat", "lon"),
        P(),
    )
    return jax.shard_map(
        on_device,
        mesh=mesh,
        in_specs=placed,
        out_specs=(P(None, "lat", "lon"), P(None, "lat", "lon"), P(None, "lat", "lon")),
        check_vma=False,
    )
```

```python
import functools

import jax
import jax.numpy as jnp
from jax import lax
from jax.experimental import pallas as pl
from jax.experimental.pallas import tpu as pltpu
from jax.sharding import PartitionSpec as P

ROWS = 4
LANES = 128
SPAN = 64
F32 = jnp.float32
BF16 = jnp.bfloat16


def iota(shape, dim):
    return lax.broadcasted_iota(jnp.int32, shape, dim)


def swap(block, axis, odd):
    count = lax.axis_size(axis)
    ends = [(i, i + 1) for i in range(odd, count - 1, 2)]
    if odd and axis == "lon":
        ends.append((count - 1, 0))
    return lax.ppermute(block, axis, ends + [(b, a) for a, b in ends])


def swaps(even_block, odd_block, axis):
    return swap(even_block, axis, 0), swap(odd_block, axis, 1)


def from_pole(block, ends):
    sectors = lax.axis_size("lon")
    pairs = [
        (source * sectors + s, band * sectors + (s + sectors // 2) % sectors)
        for source, band in ends
        for s in range(sectors)
    ]
    return lax.ppermute(block, ("lat", "lon"), pairs)


def from_far(block):
    last = lax.axis_size("lat") - 1
    return from_pole(block, ((0, 0), (last, last)))


def from_far_next(block):
    last = lax.axis_size("lat") - 1
    return from_pole(block, ((1, 0), (last - 1, last)))


def after(block, *others):
    return lax.optimization_barrier((block,) + others)[0]


def coded(depart_lists, tiles):
    bands, sectors = lax.axis_size("lat"), lax.axis_size("lon")
    band, sector = lax.axis_index("lat"), lax.axis_index("lon")
    wanted = depart_lists.transpose(1, 2, 0).reshape(1, -1)
    owner = wanted // tiles
    theirs = owner % sectors
    turn = jnp.where(theirs == (sector ^ 1), 1, 2)
    turn = jnp.where(theirs == (sector + sectors // 2) % sectors, 3, turn)
    turn = jnp.where(theirs == sector, 0, turn)
    source = owner // sectors
    place = jnp.where(source == band, 0, jnp.where(source == (band ^ 1), 1, 2))
    code = turn * SPAN + place * tiles + wanted % tiles
    return jnp.pad(code, ((0, 0), (0, LANES - code.shape[1])), constant_values=4 * SPAN)


def flat(rows):
    return pl.BlockSpec((rows, LANES), lambda g: (0, 0))


def ranks(member):
    before = (iota((LANES, LANES), 0) < iota((LANES, LANES), 1)).astype(BF16)
    ones = jnp.where(member, 1.0, 0.0).astype(BF16)
    return jnp.dot(ones, before, preferred_element_type=F32)


def pack_kernel(count, *refs):
    lists, (own, next_even, next_odd), outs, pick = refs[:count], refs[count : count + 3], refs[count + 3 : -1], refs[-1]

    @pl.when(pl.program_id(0) == 0)
    def _():
        sub = iota((8, LANES), 0)
        codes = jnp.where(sub == 0, lists[0][...], lists[1][...])
        if count > 2:
            far_codes = lists[2][0].astype(F32)[:8].astype(jnp.int32)
            codes = jnp.where(sub == 2, far_codes, codes)
        member = (codes >> 6) == sub + 1
        rank = jnp.where(member, ranks(member), -1.0)
        tile = ((codes & (SPAN - 1)) + 1).astype(F32)
        slot = (iota((64, LANES), 0) >> 2).astype(F32)
        row = (iota((64, 192), 0) & 3).astype(F32)
        col = iota((64, 192), 1).astype(F32)
        for d in range(count):
            hit = rank[d : d + 1] == slot
            held = jnp.sum(jnp.where(hit, tile[d : d + 1], 0.0), axis=1, keepdims=True) - 1.0
            pick[d * 64 : (d + 1) * 64, :] = jnp.where(col == held * 4.0 + row, 1.0, 0.0).astype(BF16)

    def pair(g, carry):
        pool = jnp.concatenate(
            [jnp.concatenate([ref[f] for ref in (own, next_even, next_odd)], axis=0) for f in (2 * g, 2 * g + 1)],
            axis=1,
        )
        got = jnp.dot(pick[...], pool, preferred_element_type=F32).astype(BF16)
        for d, out in enumerate(outs):
            for half in range(2):
                out[2 * g + half] = got[d * 64 : (d + 1) * 64, half * LANES : (half + 1) * LANES]
        return carry

    lax.fori_loop(0, 8, pair, 0, unroll=8)


def pack(lists, bands, blocks, of):
    levels, count = 16 * blocks, len(lists)
    source = pl.BlockSpec((16, 64, LANES), lambda g: (of(g), 0, 0))
    block = pl.BlockSpec((16, 64, LANES), lambda g: (g, 0, 0))
    rows = [flat(1)] * 2 + [pl.BlockSpec((1, 64, LANES), lambda g: (32, 0, 0))] * (count - 2)
    return pl.pallas_call(
        functools.partial(pack_kernel, count),
        grid=(blocks,),
        in_specs=rows + [source] * 3,
        out_specs=[block] * count,
        out_shape=[jax.ShapeDtypeStruct((levels, 64, LANES), BF16)] * count,
        scratch_shapes=[pltpu.VMEM((count * 64, 192), BF16)],
        compiler_params=pltpu.CompilerParams(vmem_limit_bytes=32 << 20),
        cost_estimate=pl.CostEstimate(
            flops=levels * 2 * 192 * 192 * LANES, bytes_accessed=levels * 5 * 64 * LANES * 2, transcendentals=0
        ),
        name="pack",
    )(*lists, *bands)


def set_gather(codes_ref, gather, far_slots):
    codes = jnp.broadcast_to(codes_ref[...], (8, LANES))
    turn = codes >> 6
    sub = iota((8, LANES), 0)
    rank = ranks(turn == sub)
    turn, tile = turn[:1], codes[:1] & (SPAN - 1)
    place = jnp.where(turn == 0, tile.astype(F32), -1.0)
    place = jnp.where(turn == 1, 48.0 + rank[1:2], place)
    place = jnp.where(turn == 2, 64.0 + rank[2:3], place)
    if far_slots:
        across = 80.0 + rank[3:4]
    else:
        across = ((tile & 15) + jnp.where(tile < 16, 80, 96)).astype(F32)
    place = jnp.where(turn == 3, across, place)
    row = iota((LANES, LANES), 0)
    mine = iota((LANES, LANES), 1) == (row & 15) + 16 * (row >> 6)
    place = jnp.sum(jnp.where(mine, place, 0.0), axis=1, keepdims=True)
    within = ((iota(gather.shape, 0) >> 4) & 3).astype(F32)
    col = iota(gather.shape, 1).astype(F32)
    gather[...] = jnp.where(col == place * 4.0 + within, 1.0, 0.0).astype(BF16)


def every_fourth(q):
    return pl.ds(q, 16, stride=4)


def set_weights(table, coef):
    for q in range(4):
        *points, offset = (table[m, every_fourth(q), :] for m in range(5))
        for r in range(8):
            value = jnp.zeros((16, LANES), F32)
            for m in range(4):
                if 0 <= r - m <= 4:
                    value = jnp.where(offset == float(r - m), points[m], value)
            coef[q * 8 + r] = value


def interpolate(gather, coef, first_pools, second_pools, first, second=None):
    second = first if second is None else second
    pool = jnp.concatenate(
        [
            jnp.concatenate([ref[f] for ref in pools], axis=0)
            for pools, f in ((first_pools, first), (second_pools, second))
        ],
        axis=1,
    )
    rows = jnp.dot(gather[...], pool, preferred_element_type=F32)
    out = []
    for q in range(4):
        sums = [None, None]
        for r in range(8):
            weight = coef[q * 8 + r]
            for h in range(2):
                term = weight * rows[r * 16 : (r + 1) * 16, h * LANES : (h + 1) * LANES]
                sums[h] = term if r == 0 else sums[h] + term
        out.append(sums)
    return out


def levels_block(of):
    return pl.BlockSpec((16, 64, LANES), lambda g: (of(g), 0, 0))


SMEM = pl.BlockSpec(memory_space=pltpu.SMEM)
VMEM = pl.BlockSpec(memory_space=pltpu.VMEM)
TABLE = pl.BlockSpec((5, 64, LANES), lambda g: (0, 0, 0))


def scratch(pool):
    return [
        pltpu.VMEM((LANES, 64 * pool), BF16), pltpu.VMEM((32, 16, LANES), F32), pltpu.VMEM((16, 64, LANES), F32)
    ]


def first_kernel(scale, codes, table, diag, *refs):
    middle, top = refs[0:7], refs[7:14]
    adv, rhs, cols, edge_even, edge_odd, gather, coef, tmp, own_up, own_down = refs[14:]
    set_gather(codes, gather, False)
    set_weights(table, coef)

    def level(l, carry):
        values = interpolate(gather, coef, middle, top, l)
        for q in range(4):
            tmp[l, every_fourth(q), :] = values[q][0]
            rhs[l, every_fourth(q), :] = values[q][1] + 0.5 * values[q][0]
        return carry

    lax.fori_loop(0, 16, level, 0, unroll=16)
    group = iota((64, LANES), 1) >> 2
    packed = jnp.where(group == 16, pltpu.roll(diag[...], 65, 1), 0.0)
    for l in range(16):
        adv[l] = tmp[l].astype(BF16)
        value = rhs[l] / (4.0 + diag[...] * scale[l])
        for ref, ends in ((own_up, (0, 1)), (own_down, (63, 62))):
            for place, r in enumerate(ends):
                ref[16 * place + l : 16 * place + l + 1, :] = value[r : r + 1]
        packed = jnp.where(group == l, pltpu.roll(value, 2 + 4 * l, 1), packed)
    cols[...] = packed
    for ref, r in ((own_up, 0), (own_down, 63)):
        ref[32:33, :] = diag[r : r + 1, :]
        ref[33:40, :] = jnp.ones((7, LANES), F32)
    up, down = own_up[...], own_down[...]
    even_band = lax.rem(lax.axis_index("lat"), 2) == 0
    edge_even[...] = jnp.where(even_band, down, up)
    edge_odd[...] = jnp.where(even_band, up, down)


def first_levels(scale, codes, table, diag, bands, slots, far):
    slab = jax.ShapeDtypeStruct((16, 64, LANES), F32)
    edge = jax.ShapeDtypeStruct((40, LANES), F32)
    whole = levels_block(lambda g: 0)
    pools, specs = [], []
    for half in range(2):
        pools += [*bands, *slots, *far]
        specs += [levels_block(lambda g, half=half: 2 + 2 * half)] * 3 + [levels_block(lambda g, half=half: half)] * 4
    return pl.pallas_call(
        first_kernel,
        grid=(1,),
        in_specs=[SMEM, flat(1), TABLE, flat(64)] + specs,
        out_specs=[levels_block(lambda g: 2), whole, flat(64)] + [flat(40)] * 2,
        out_shape=[
            jax.ShapeDtypeStruct((64, 64, LANES), BF16), slab, jax.ShapeDtypeStruct((64, LANES), F32)
        ] + [edge] * 2,
        scratch_shapes=scratch(7) + [pltpu.VMEM((40, LANES), F32)] * 2,
        compiler_params=pltpu.CompilerParams(vmem_limit_bytes=32 << 20),
        cost_estimate=pl.CostEstimate(flops=32 * 2 * 128 * 448 * 128, bytes_accessed=6 << 20, transcendentals=0),
        name="first_levels",
    )(scale, codes, table, diag, *pools)


def other_kernel(codes, table, *refs):
    pools, (start, adv, gather, coef, tmp) = refs[:6], refs[6:]

    @pl.when(pl.program_id(0) == 0)
    def _():
        set_gather(codes, gather, True)
        set_weights(table, coef)

    def pair(g, carry):
        values = interpolate(gather, coef, pools, pools, 2 * g, 2 * g + 1)
        for h in range(2):
            for q in range(4):
                tmp[2 * g + h, every_fourth(q), :] = values[q][h]
        return carry

    lax.fori_loop(0, 8, pair, 0, unroll=8)
    for f in range(16):
        adv[f] = tmp[f].astype(BF16)


def other_levels(codes, table, bands, slots, start):
    return pl.pallas_call(
        other_kernel,
        grid=(3,),
        in_specs=[flat(1), TABLE]
        + [levels_block(lambda g: g + g // 2)] * 3
        + [levels_block(lambda g: g)] * 3
        + [pl.BlockSpec(memory_space=pl.ANY)],
        out_specs=levels_block(lambda g: g + g // 2),
        out_shape=jax.ShapeDtypeStruct(start.shape, start.dtype),
        scratch_shapes=scratch(6),
        input_output_aliases={8: 0},
        compiler_params=pltpu.CompilerParams(vmem_limit_bytes=32 << 20),
        cost_estimate=pl.CostEstimate(flops=48 * 2 * 128 * 448 * 128, bytes_accessed=6 << 20, transcendentals=0),
        name="other_levels",
    )(codes, table, *bands, *slots, start)


def sum_kernel(scale, rhs, diag, cols, cols_even, cols_odd, edge_even, edge_odd, n0, n1, sums, rowsums):
    lane = iota((64, LANES), 1)
    even_band = lax.rem(lax.axis_index("lat"), 2) == 0
    even_sector = lax.rem(lax.axis_index("lon"), 2) == 0
    even, odd = edge_even[...], edge_odd[...]
    above, below = jnp.where(even_band, odd, even), jnp.where(even_band, even, odd)
    even, odd = cols_even[...], cols_odd[...]
    left, right = jnp.where(even_sector, odd, even), jnp.where(even_sector, even, odd)
    spread = jnp.zeros((1, LANES), F32)
    column = jnp.zeros((16, LANES), F32)
    for l in range(16):
        spread = jnp.where((lane[:1] >> 2) == l, scale[l], spread)
        column = jnp.where(iota((16, LANES), 0) == l, scale[l], column)
    row16, lane16 = iota((16, LANES), 0), lane[:16]

    west_even, west_odd = left[64:80, LANES - 1 : LANES], left[80:96, LANES - 1 : LANES]
    east_even, east_odd = right[64:80, 0:1], right[80:96, 0:1]
    corners = [
        [jnp.where(even_band, west_odd, west_even), jnp.where(even_band, east_odd, east_even)],
        [jnp.where(even_band, west_even, west_odd), jnp.where(even_band, east_even, east_odd)],
    ]

    def spread_corner(column, which):
        return jnp.sum(jnp.where(lane16 == 4 * row16 + which, column, 0.0), axis=0, keepdims=True)

    def rim_row(edge, inner, west, east):
        near, second, flag = edge[0:16, :], edge[16:32, :], edge[33:34, :]
        beside = jnp.where(lane16 == 0, west, pltpu.roll(near, 1, 1))
        beside = beside + jnp.where(lane16 == LANES - 1, east, pltpu.roll(near, LANES - 1, 1))
        return flag * (second + inner + beside) / (4.0 + edge[32:33, :] * column)

    def own_row(r):
        rows = jnp.concatenate([rhs[l, r : r + 1, :] for l in range(16)], axis=0)
        return rows / (4.0 + diag[r : r + 1, :] * column)

    top, bottom = rim_row(above, own_row(0), *corners[0]), rim_row(below, own_row(63), *corners[1])

    def rim_col(edge, side, which, toward, diag_lane):
        values = edge[0:64]
        first, last = (spread_corner(pair[side], which) for pair in corners)
        up = jnp.concatenate([first, values[:-1]], axis=0)
        down = jnp.concatenate([values[1:], last], axis=0)
        outer = pltpu.roll(values, toward % LANES, 1)
        inner = pltpu.roll(cols[...], -toward % LANES, 1)
        coef = 4.0 + values[:, diag_lane : diag_lane + 1] * spread
        return (up + down + outer + inner) / coef

    west = rim_col(left, 0, 1, 1, 64)
    east = rim_col(right, 1, 2, -1, 65)

    def beside(value, west_col, east_col, upper, lower):
        total = jnp.where(lane == 0, west_col, pltpu.roll(value, 1, 1))
        total = total + jnp.where(lane == LANES - 1, east_col, pltpu.roll(value, LANES - 1, 1))
        total = total + jnp.concatenate([upper, value[:-1]], axis=0)
        return total + jnp.concatenate([value[1:], lower], axis=0)

    for l in range(16):
        start = rhs[l]
        inverse = 1.0 / (4.0 + diag[...] * scale[l])
        value = start * inverse
        around = beside(
            value, left[0:64, 4 * l + 1 : 4 * l + 2], right[0:64, 4 * l + 2 : 4 * l + 3], above[l : l + 1, :], below[l : l + 1, :]
        )
        n0[l] = around
        again = around * inverse
        second = beside(
            again, west[:, 4 * l + 1 : 4 * l + 2], east[:, 4 * l + 2 : 4 * l + 3], top[l : l + 1], bottom[l : l + 1]
        )
        n1[l] = second
        for k, term in enumerate((start * value, start * again, around * again, second * again)):
            part = term[0:8]
            for j in range(1, 8):
                part = part + term[8 * j : 8 * j + 8]
            rowsums[k * 16 + l : k * 16 + l + 1, :] = jnp.sum(part, axis=0, keepdims=True)
    total = jnp.sum(rowsums[...], axis=1, keepdims=True)
    packed = jnp.sum(jnp.where(lane == iota((64, LANES), 0), total, 0.0), axis=0, keepdims=True)
    for j in range(sums.shape[0]):
        sums[j] = packed


def level_sums(scale, rhs, diag, cols, cols_rim, edges):
    slab = jax.ShapeDtypeStruct((16, 64, LANES), F32)
    return pl.pallas_call(
        sum_kernel,
        in_specs=[SMEM] + [VMEM] * 7,
        out_specs=[VMEM] * 3,
        out_shape=[slab, slab, jax.ShapeDtypeStruct((lax.axis_size("lat"), 1, LANES), F32)],
        scratch_shapes=[pltpu.VMEM((64, LANES), F32)],
        compiler_params=pltpu.CompilerParams(vmem_limit_bytes=60 << 20),
        cost_estimate=pl.CostEstimate(flops=1 << 22, bytes_accessed=2 << 20, transcendentals=0),
        name="level_sums",
    )(scale, rhs, diag, cols, *cols_rim, *edges)


def last_kernel(scale, parts, rhs, diag, n0, n1, pressure, residual):
    total = parts[0]
    for j in range(1, parts.shape[0]):
        total = total + parts[j]
    total = jnp.broadcast_to(total, (8, LANES))
    lane, row = iota((8, LANES), 1), iota((8, LANES), 0)

    def of(k, half):
        return jnp.sum(jnp.where(lane == 16 * k + 8 * half + row, total, 0.0), axis=1, keepdims=True)

    half = pl.program_id(0)
    s0, s1, s2, s3 = (of(k, half) for k in range(4))
    curve = s0 - s1
    step = s0 / curve
    keep = -s1 / curve
    norm = keep * keep * s0 + 2.0 * keep * step * s1 + step * step * s2
    ratio = norm / s0
    bend = norm - (keep * keep * s1 + 2.0 * keep * step * s2 + step * step * s3)
    other = norm / (bend - ratio * ratio * curve)
    along = other * (keep + ratio)
    across = other * step
    fit_z, fit_p = step + along, across
    fit_r, fit_n0, fit_n1 = keep - along, step + along - across, across
    for s in range(8):
        at = lambda column: column[s : s + 1]
        inverse = 1.0 / (4.0 + diag[...] * scale[8 * half + s])
        start, around = rhs[s], n0[s]
        pressure[s] = (at(fit_z) * start + at(fit_p) * around) * inverse
        residual[s] = at(fit_r) * start + at(fit_n0) * around + at(fit_n1) * n1[s]


def last_step(scale, parts, rhs, diag, n0, n1):
    slab = jax.ShapeDtypeStruct((16, 64, LANES), F32)
    block = pl.BlockSpec((8, 64, LANES), lambda g: (g, 0, 0))
    return pl.pallas_call(
        last_kernel,
        grid=(2,),
        in_specs=[SMEM, pl.BlockSpec(parts.shape, lambda g: (0, 0, 0)), block, flat(64), block, block],
        out_specs=[block] * 2,
        out_shape=[slab, slab],
        input_output_aliases={2: 1, 4: 0},
        compiler_params=pltpu.CompilerParams(vmem_limit_bytes=60 << 20),
        cost_estimate=pl.CostEstimate(flops=1 << 21, bytes_accessed=3 << 20, transcendentals=0),
        name="last_step",
    )(scale, parts, rhs, diag, n0, n1)


def exchange(parts, axis):
    return lax.all_to_all(parts, axis, split_axis=0, concat_axis=0, tiled=True)


def on_device(fields, depart_lists, stencil_offsets, interp_weights, diag_coef, level_scale):
    tiles = depart_lists.shape[0]
    codes = coded(depart_lists, tiles)
    bands = (fields,) + swaps(fields, fields, "lat")
    lists = swaps(codes, codes, "lon")
    rows = jnp.broadcast_to(codes.astype(BF16)[None], (1, 64, LANES))
    first = after(jnp.concatenate([fields[32:48], fields[64:80], rows], axis=0), *lists)
    first_far = (from_far(first), from_far_next(first))
    first_out = pack(lists, bands, 2, lambda g: 2 + 2 * g)
    first_slots = swaps(*first_out, "lon")
    later = after(lists[0], *first_out, *first_far)
    offsets = after(stencil_offsets, *first_out)
    table = jnp.concatenate([interp_weights, offsets.astype(F32)[None]], axis=0)
    *other_out, other_far = pack((later, lists[1], first_far[0]), bands, 3, lambda g: g + g // 2)
    other_slots = swaps(*other_out, "lon")
    first_slots = (after(first_slots[0], *other_out), first_slots[1])
    adv, rhs, cols, *edges = first_levels(
        level_scale, codes, table, diag_coef, bands, first_slots, first_far
    )
    edges = swaps(*edges, "lat")
    rim = jnp.concatenate([cols, edges[0][:16], edges[1][:16]], axis=0)
    cols_rim = swaps(rim, rim, "lon")
    other_far = from_far(after(other_far, *cols_rim))
    n0, n1, parts = level_sums(level_scale, rhs, diag_coef, cols, cols_rim, edges)
    parts = jnp.sum(exchange(parts, "lat"), axis=0)
    parts = exchange(jnp.broadcast_to(parts[None], (lax.axis_size("lon"),) + parts.shape), "lon")
    adv = other_levels(codes, table, bands, other_slots + (other_far,), adv)
    parts = after(parts, adv)
    pressure, residual = last_step(level_scale, parts, rhs, diag_coef, n0, n1)
    return (adv, pressure, residual)


def solution(mesh):
    placed = (
        P(None, "lat", "lon"),
        P("lat", "lon", None),
        P("lat", "lon"),
        P(None, "lat", "lon"),
        P("lat", "lon"),
        P(),
    )
    return jax.shard_map(
        on_device,
        mesh=mesh,
        in_specs=placed,
        out_specs=(P(None, "lat", "lon"), P(None, "lat", "lon"), P(None, "lat", "lon")),
        check_vma=False,
    )
```

```python
import functools

import jax
import jax.numpy as jnp
from jax import lax
from jax.experimental import pallas as pl
from jax.experimental.pallas import tpu as pltpu
from jax.sharding import PartitionSpec as P

ROWS = 4
LANES = 128
SPAN = 64
F32 = jnp.float32
BF16 = jnp.bfloat16


def iota(shape, dim):
    return lax.broadcasted_iota(jnp.int32, shape, dim)


def swap(block, axis, odd):
    count = lax.axis_size(axis)
    ends = [(i, i + 1) for i in range(odd, count - 1, 2)]
    if odd and axis == "lon":
        ends.append((count - 1, 0))
    return lax.ppermute(block, axis, ends + [(b, a) for a, b in ends])


def swaps(even_block, odd_block, axis):
    return swap(even_block, axis, 0), swap(odd_block, axis, 1)


def from_pole(block, ends):
    sectors = lax.axis_size("lon")
    pairs = [
        (source * sectors + s, band * sectors + (s + sectors // 2) % sectors)
        for source, band in ends
        for s in range(sectors)
    ]
    return lax.ppermute(block, ("lat", "lon"), pairs)


def from_far(block):
    last = lax.axis_size("lat") - 1
    return from_pole(block, ((0, 0), (last, last)))


def from_far_next(block):
    last = lax.axis_size("lat") - 1
    return from_pole(block, ((1, 0), (last - 1, last)))


def after(block, *others):
    return lax.optimization_barrier((block,) + others)[0]


def coded(depart_lists, tiles):
    bands, sectors = lax.axis_size("lat"), lax.axis_size("lon")
    band, sector = lax.axis_index("lat"), lax.axis_index("lon")
    wanted = depart_lists.transpose(1, 2, 0).reshape(1, -1)
    owner = wanted // tiles
    theirs = owner % sectors
    turn = jnp.where(theirs == (sector ^ 1), 1, 2)
    turn = jnp.where(theirs == (sector + sectors // 2) % sectors, 3, turn)
    turn = jnp.where(theirs == sector, 0, turn)
    source = owner // sectors
    place = jnp.where(source == band, 0, jnp.where(source == (band ^ 1), 1, 2))
    code = turn * SPAN + place * tiles + wanted % tiles
    return jnp.pad(code, ((0, 0), (0, LANES - code.shape[1])), constant_values=4 * SPAN)


def flat(rows):
    return pl.BlockSpec((rows, LANES), lambda g: (0, 0))


def ranks(member):
    before = (iota((LANES, LANES), 0) < iota((LANES, LANES), 1)).astype(BF16)
    ones = jnp.where(member, 1.0, 0.0).astype(BF16)
    return jnp.dot(ones, before, preferred_element_type=F32)


def pack_kernel(count, *refs):
    lists, (own, next_even, next_odd), outs, pick = refs[:count], refs[count : count + 3], refs[count + 3 : -1], refs[-1]

    @pl.when(pl.program_id(0) == 0)
    def _():
        sub = iota((8, LANES), 0)
        codes = jnp.where(sub == 0, lists[0][...], lists[1][...])
        if count > 2:
            far_codes = lists[2][0].astype(F32)[:8].astype(jnp.int32)
            codes = jnp.where(sub == 2, far_codes, codes)
        member = (codes >> 6) == sub + 1
        rank = jnp.where(member, ranks(member), -1.0)
        tile = ((codes & (SPAN - 1)) + 1).astype(F32)
        slot = (iota((64, LANES), 0) >> 2).astype(F32)
        row = (iota((64, 192), 0) & 3).astype(F32)
        col = iota((64, 192), 1).astype(F32)
        for d in range(count):
            hit = rank[d : d + 1] == slot
            held = jnp.sum(jnp.where(hit, tile[d : d + 1], 0.0), axis=1, keepdims=True) - 1.0
            pick[d * 64 : (d + 1) * 64, :] = jnp.where(col == held * 4.0 + row, 1.0, 0.0).astype(BF16)

    def pair(g, carry):
        pool = jnp.concatenate(
            [jnp.concatenate([ref[f] for ref in (own, next_even, next_odd)], axis=0) for f in (2 * g, 2 * g + 1)],
            axis=1,
        )
        got = jnp.dot(pick[...], pool, preferred_element_type=F32).astype(BF16)
        for d, out in enumerate(outs):
            for half in range(2):
                out[2 * g + half] = got[d * 64 : (d + 1) * 64, half * LANES : (half + 1) * LANES]
        return carry

    lax.fori_loop(0, 8, pair, 0, unroll=8)


def pack(lists, bands, blocks, of):
    levels, count = 16 * blocks, len(lists)
    source = pl.BlockSpec((16, 64, LANES), lambda g: (of(g), 0, 0))
    block = pl.BlockSpec((16, 64, LANES), lambda g: (g, 0, 0))
    rows = [flat(1)] * 2 + [pl.BlockSpec((1, 64, LANES), lambda g: (32, 0, 0))] * (count - 2)
    return pl.pallas_call(
        functools.partial(pack_kernel, count),
        grid=(blocks,),
        in_specs=rows + [source] * 3,
        out_specs=[block] * count,
        out_shape=[jax.ShapeDtypeStruct((levels, 64, LANES), BF16)] * count,
        scratch_shapes=[pltpu.VMEM((count * 64, 192), BF16)],
        compiler_params=pltpu.CompilerParams(vmem_limit_bytes=32 << 20),
        cost_estimate=pl.CostEstimate(
            flops=levels * 2 * 192 * 192 * LANES, bytes_accessed=levels * 5 * 64 * LANES * 2, transcendentals=0
        ),
        name="pack",
    )(*lists, *bands)


def set_gather(codes_ref, gather, far_slots):
    codes = jnp.broadcast_to(codes_ref[...], (8, LANES))
    turn = codes >> 6
    sub = iota((8, LANES), 0)
    rank = ranks(turn == sub)
    turn, tile = turn[:1], codes[:1] & (SPAN - 1)
    place = jnp.where(turn == 0, tile.astype(F32), -1.0)
    even_at, odd_at = (64.0, 48.0) if far_slots else (48.0, 64.0)
    place = jnp.where(turn == 1, even_at + rank[1:2], place)
    place = jnp.where(turn == 2, odd_at + rank[2:3], place)
    if far_slots:
        across = 80.0 + rank[3:4]
    else:
        across = ((tile & 15) + jnp.where(tile < 16, 80, 96)).astype(F32)
    place = jnp.where(turn == 3, across, place)
    row = iota((LANES, LANES), 0)
    mine = iota((LANES, LANES), 1) == (row & 15) + 16 * (row >> 6)
    place = jnp.sum(jnp.where(mine, place, 0.0), axis=1, keepdims=True)
    within = ((iota(gather.shape, 0) >> 4) & 3).astype(F32)
    col = iota(gather.shape, 1).astype(F32)
    gather[...] = jnp.where(col == place * 4.0 + within, 1.0, 0.0).astype(BF16)


def every_fourth(q):
    return pl.ds(q, 16, stride=4)


def set_weights(table, coef):
    for q in range(4):
        *points, offset = (table[m, every_fourth(q), :] for m in range(5))
        for r in range(8):
            value = jnp.zeros((16, LANES), F32)
            for m in range(4):
                if 0 <= r - m <= 4:
                    value = jnp.where(offset == float(r - m), points[m], value)
            coef[q * 8 + r] = value


def interpolate(gather, coef, first_pools, second_pools, first, second=None):
    second = first if second is None else second
    pool = jnp.concatenate(
        [
            jnp.concatenate([ref[f] for ref in pools], axis=0)
            for pools, f in ((first_pools, first), (second_pools, second))
        ],
        axis=1,
    )
    rows = jnp.dot(gather[...], pool, preferred_element_type=F32)
    out = []
    for q in range(4):
        sums = [None, None]
        for r in range(8):
            weight = coef[q * 8 + r]
            for h in range(2):
                term = weight * rows[r * 16 : (r + 1) * 16, h * LANES : (h + 1) * LANES]
                sums[h] = term if r == 0 else sums[h] + term
        out.append(sums)
    return out


def levels_block(of):
    return pl.BlockSpec((16, 64, LANES), lambda g: (of(g), 0, 0))


SMEM = pl.BlockSpec(memory_space=pltpu.SMEM)
VMEM = pl.BlockSpec(memory_space=pltpu.VMEM)
TABLE = pl.BlockSpec((5, 64, LANES), lambda g: (0, 0, 0))


def scratch(pool):
    return [
        pltpu.VMEM((LANES, 64 * pool), BF16), pltpu.VMEM((32, 16, LANES), F32), pltpu.VMEM((16, 64, LANES), F32)
    ]


def first_kernel(scale, codes, table, diag, *refs):
    middle, top = refs[0:7], refs[7:14]
    adv, rhs, cols, edge_even, edge_odd, gather, coef, tmp, own_up, own_down = refs[14:]
    set_gather(codes, gather, False)
    set_weights(table, coef)

    def level(l, carry):
        values = interpolate(gather, coef, middle, top, l)
        for q in range(4):
            tmp[l, every_fourth(q), :] = values[q][0]
            rhs[l, every_fourth(q), :] = values[q][1] + 0.5 * values[q][0]
        return carry

    lax.fori_loop(0, 16, level, 0, unroll=16)
    group = iota((64, LANES), 1) >> 2
    packed = jnp.where(group == 16, pltpu.roll(diag[...], 65, 1), 0.0)
    for l in range(16):
        adv[l] = tmp[l].astype(BF16)
        value = rhs[l] / (4.0 + diag[...] * scale[l])
        for ref, ends in ((own_up, (0, 1)), (own_down, (63, 62))):
            for place, r in enumerate(ends):
                ref[16 * place + l : 16 * place + l + 1, :] = value[r : r + 1]
        packed = jnp.where(group == l, pltpu.roll(value, 2 + 4 * l, 1), packed)
    cols[...] = packed
    for ref, r in ((own_up, 0), (own_down, 63)):
        ref[32:33, :] = diag[r : r + 1, :]
        ref[33:40, :] = jnp.ones((7, LANES), F32)
    up, down = own_up[...], own_down[...]
    even_band = lax.rem(lax.axis_index("lat"), 2) == 0
    edge_even[...] = jnp.where(even_band, down, up)
    edge_odd[...] = jnp.where(even_band, up, down)


def first_levels(scale, codes, table, diag, bands, slots, far):
    slab = jax.ShapeDtypeStruct((16, 64, LANES), F32)
    edge = jax.ShapeDtypeStruct((40, LANES), F32)
    whole = levels_block(lambda g: 0)
    pools, specs = [], []
    for half in range(2):
        pools += [*bands, *slots, *far]
        specs += [levels_block(lambda g, half=half: 2 + 2 * half)] * 3 + [levels_block(lambda g, half=half: half)] * 4
    return pl.pallas_call(
        first_kernel,
        grid=(1,),
        in_specs=[SMEM, flat(1), TABLE, flat(64)] + specs,
        out_specs=[levels_block(lambda g: 2), whole, flat(64)] + [flat(40)] * 2,
        out_shape=[
            jax.ShapeDtypeStruct((64, 64, LANES), BF16), slab, jax.ShapeDtypeStruct((64, LANES), F32)
        ] + [edge] * 2,
        scratch_shapes=scratch(7) + [pltpu.VMEM((40, LANES), F32)] * 2,
        compiler_params=pltpu.CompilerParams(vmem_limit_bytes=32 << 20),
        cost_estimate=pl.CostEstimate(flops=32 * 2 * 128 * 448 * 128, bytes_accessed=6 << 20, transcendentals=0),
        name="first_levels",
    )(scale, codes, table, diag, *pools)


def other_kernel(codes, table, *refs):
    pools, (start, adv, gather, coef, tmp) = refs[:6], refs[6:]

    @pl.when(pl.program_id(0) == 0)
    def _():
        set_gather(codes, gather, True)
        set_weights(table, coef)

    def pair(g, carry):
        values = interpolate(gather, coef, pools, pools, 2 * g, 2 * g + 1)
        for h in range(2):
            for q in range(4):
                tmp[2 * g + h, every_fourth(q), :] = values[q][h]
        return carry

    lax.fori_loop(0, 8, pair, 0, unroll=8)
    for f in range(16):
        adv[f] = tmp[f].astype(BF16)


def other_levels(codes, table, bands, slots, start):
    return pl.pallas_call(
        other_kernel,
        grid=(3,),
        in_specs=[flat(1), TABLE]
        + [levels_block(lambda g: g + g // 2)] * 3
        + [levels_block(lambda g: g)] * 3
        + [pl.BlockSpec(memory_space=pl.ANY)],
        out_specs=levels_block(lambda g: g + g // 2),
        out_shape=jax.ShapeDtypeStruct(start.shape, start.dtype),
        scratch_shapes=scratch(6),
        input_output_aliases={8: 0},
        compiler_params=pltpu.CompilerParams(vmem_limit_bytes=32 << 20),
        cost_estimate=pl.CostEstimate(flops=48 * 2 * 128 * 448 * 128, bytes_accessed=6 << 20, transcendentals=0),
        name="other_levels",
    )(codes, table, *bands, *slots, start)


def sum_kernel(scale, rhs, diag, cols, cols_even, cols_odd, edge_even, edge_odd, n0, n1, sums, rowsums):
    lane = iota((64, LANES), 1)
    even_band = lax.rem(lax.axis_index("lat"), 2) == 0
    even_sector = lax.rem(lax.axis_index("lon"), 2) == 0
    even, odd = edge_even[...], edge_odd[...]
    above, below = jnp.where(even_band, odd, even), jnp.where(even_band, even, odd)
    even, odd = cols_even[...], cols_odd[...]
    left, right = jnp.where(even_sector, odd, even), jnp.where(even_sector, even, odd)
    spread = jnp.zeros((1, LANES), F32)
    column = jnp.zeros((16, LANES), F32)
    for l in range(16):
        spread = jnp.where((lane[:1] >> 2) == l, scale[l], spread)
        column = jnp.where(iota((16, LANES), 0) == l, scale[l], column)
    row16, lane16 = iota((16, LANES), 0), lane[:16]

    west_even, west_odd = left[64:80, LANES - 1 : LANES], left[80:96, LANES - 1 : LANES]
    east_even, east_odd = right[64:80, 0:1], right[80:96, 0:1]
    corners = [
        [jnp.where(even_band, west_odd, west_even), jnp.where(even_band, east_odd, east_even)],
        [jnp.where(even_band, west_even, west_odd), jnp.where(even_band, east_even, east_odd)],
    ]

    def spread_corner(column, which):
        return jnp.sum(jnp.where(lane16 == 4 * row16 + which, column, 0.0), axis=0, keepdims=True)

    def rim_row(edge, inner, west, east):
        near, second, flag = edge[0:16, :], edge[16:32, :], edge[33:34, :]
        beside = jnp.where(lane16 == 0, west, pltpu.roll(near, 1, 1))
        beside = beside + jnp.where(lane16 == LANES - 1, east, pltpu.roll(near, LANES - 1, 1))
        return flag * (second + inner + beside) / (4.0 + edge[32:33, :] * column)

    def own_row(r):
        rows = jnp.concatenate([rhs[l, r : r + 1, :] for l in range(16)], axis=0)
        return rows / (4.0 + diag[r : r + 1, :] * column)

    top, bottom = rim_row(above, own_row(0), *corners[0]), rim_row(below, own_row(63), *corners[1])

    def rim_col(edge, side, which, toward, diag_lane):
        values = edge[0:64]
        first, last = (spread_corner(pair[side], which) for pair in corners)
        up = jnp.concatenate([first, values[:-1]], axis=0)
        down = jnp.concatenate([values[1:], last], axis=0)
        outer = pltpu.roll(values, toward % LANES, 1)
        inner = pltpu.roll(cols[...], -toward % LANES, 1)
        coef = 4.0 + values[:, diag_lane : diag_lane + 1] * spread
        return (up + down + outer + inner) / coef

    west = rim_col(left, 0, 1, 1, 64)
    east = rim_col(right, 1, 2, -1, 65)

    def beside(value, west_col, east_col, upper, lower):
        total = jnp.where(lane == 0, west_col, pltpu.roll(value, 1, 1))
        total = total + jnp.where(lane == LANES - 1, east_col, pltpu.roll(value, LANES - 1, 1))
        total = total + jnp.concatenate([upper, value[:-1]], axis=0)
        return total + jnp.concatenate([value[1:], lower], axis=0)

    for l in range(16):
        start = rhs[l]
        inverse = 1.0 / (4.0 + diag[...] * scale[l])
        value = start * inverse
        around = beside(
            value, left[0:64, 4 * l + 1 : 4 * l + 2], right[0:64, 4 * l + 2 : 4 * l + 3], above[l : l + 1, :], below[l : l + 1, :]
        )
        n0[l] = around
        again = around * inverse
        second = beside(
            again, west[:, 4 * l + 1 : 4 * l + 2], east[:, 4 * l + 2 : 4 * l + 3], top[l : l + 1], bottom[l : l + 1]
        )
        n1[l] = second
        for k, term in enumerate((start * value, start * again, around * again, second * again)):
            part = term[0:8]
            for j in range(1, 8):
                part = part + term[8 * j : 8 * j + 8]
            rowsums[k * 16 + l : k * 16 + l + 1, :] = jnp.sum(part, axis=0, keepdims=True)
    total = jnp.sum(rowsums[...], axis=1, keepdims=True)
    packed = jnp.sum(jnp.where(lane == iota((64, LANES), 0), total, 0.0), axis=0, keepdims=True)
    for j in range(sums.shape[0]):
        sums[j] = packed


def level_sums(scale, rhs, diag, cols, cols_rim, edges):
    slab = jax.ShapeDtypeStruct((16, 64, LANES), F32)
    return pl.pallas_call(
        sum_kernel,
        in_specs=[SMEM] + [VMEM] * 7,
        out_specs=[VMEM] * 3,
        out_shape=[slab, slab, jax.ShapeDtypeStruct((lax.axis_size("lat"), 1, LANES), F32)],
        scratch_shapes=[pltpu.VMEM((64, LANES), F32)],
        compiler_params=pltpu.CompilerParams(vmem_limit_bytes=60 << 20),
        cost_estimate=pl.CostEstimate(flops=1 << 22, bytes_accessed=2 << 20, transcendentals=0),
        name="level_sums",
    )(scale, rhs, diag, cols, *cols_rim, *edges)


def last_kernel(scale, parts, rhs, diag, n0, n1, pressure, residual):
    total = parts[0]
    for j in range(1, parts.shape[0]):
        total = total + parts[j]
    total = jnp.broadcast_to(total, (8, LANES))
    lane, row = iota((8, LANES), 1), iota((8, LANES), 0)

    def of(k, half):
        return jnp.sum(jnp.where(lane == 16 * k + 8 * half + row, total, 0.0), axis=1, keepdims=True)

    half = pl.program_id(0)
    s0, s1, s2, s3 = (of(k, half) for k in range(4))
    curve = s0 - s1
    step = s0 / curve
    keep = -s1 / curve
    norm = keep * keep * s0 + 2.0 * keep * step * s1 + step * step * s2
    ratio = norm / s0
    bend = norm - (keep * keep * s1 + 2.0 * keep * step * s2 + step * step * s3)
    other = norm / (bend - ratio * ratio * curve)
    along = other * (keep + ratio)
    across = other * step
    fit_z, fit_p = step + along, across
    fit_r, fit_n0, fit_n1 = keep - along, step + along - across, across
    for s in range(8):
        at = lambda column: column[s : s + 1]
        inverse = 1.0 / (4.0 + diag[...] * scale[8 * half + s])
        start, around = rhs[s], n0[s]
        pressure[s] = (at(fit_z) * start + at(fit_p) * around) * inverse
        residual[s] = at(fit_r) * start + at(fit_n0) * around + at(fit_n1) * n1[s]


def last_step(scale, parts, rhs, diag, n0, n1):
    slab = jax.ShapeDtypeStruct((16, 64, LANES), F32)
    block = pl.BlockSpec((8, 64, LANES), lambda g: (g, 0, 0))
    return pl.pallas_call(
        last_kernel,
        grid=(2,),
        in_specs=[SMEM, pl.BlockSpec(parts.shape, lambda g: (0, 0, 0)), block, flat(64), block, block],
        out_specs=[block] * 2,
        out_shape=[slab, slab],
        input_output_aliases={2: 1, 4: 0},
        compiler_params=pltpu.CompilerParams(vmem_limit_bytes=60 << 20),
        cost_estimate=pl.CostEstimate(flops=1 << 21, bytes_accessed=3 << 20, transcendentals=0),
        name="last_step",
    )(scale, parts, rhs, diag, n0, n1)


def exchange(parts, axis):
    return lax.all_to_all(parts, axis, split_axis=0, concat_axis=0, tiled=True)


def on_device(fields, depart_lists, stencil_offsets, interp_weights, diag_coef, level_scale):
    tiles = depart_lists.shape[0]
    codes = coded(depart_lists, tiles)
    bands = (fields,) + swaps(fields, fields, "lat")
    lists = swaps(codes, codes, "lon")
    rows = jnp.broadcast_to(codes.astype(BF16)[None], (1, 64, LANES))
    first = after(jnp.concatenate([fields[32:48], fields[64:80], rows], axis=0), *lists)
    first_far = (from_far(first), from_far_next(first))
    first_out = pack(lists, bands, 2, lambda g: 2 + 2 * g)
    first_slots = swaps(*first_out, "lon")
    later = after(lists[0], *first_out, *first_far)
    offsets = after(stencil_offsets, *first_out)
    table = jnp.concatenate([interp_weights, offsets.astype(F32)[None]], axis=0)
    *other_out, other_far = pack((later, lists[1], first_far[0]), bands, 3, lambda g: g + g // 2)
    other_slots = swaps(*other_out, "lon")
    first_slots = (after(first_slots[0], *other_out), first_slots[1])
    adv, rhs, cols, *edges = first_levels(
        level_scale, codes, table, diag_coef, bands, first_slots, first_far
    )
    edges = swaps(*edges, "lat")
    rim = jnp.concatenate([cols, edges[0][:16], edges[1][:16]], axis=0)
    cols_rim = swaps(rim, rim, "lon")
    other_far = from_far(after(other_far, *cols_rim))
    n0, n1, parts = level_sums(level_scale, rhs, diag_coef, cols, cols_rim, edges)
    parts = jnp.sum(exchange(parts, "lat"), axis=0)
    parts = exchange(jnp.broadcast_to(parts[None], (lax.axis_size("lon"),) + parts.shape), "lon")
    adv = other_levels(codes, table, bands, (other_slots[1], other_slots[0], other_far), adv)
    parts = after(parts, adv)
    pressure, residual = last_step(level_scale, parts, rhs, diag_coef, n0, n1)
    return (adv, pressure, residual)


def solution(mesh):
    placed = (
        P(None, "lat", "lon"),
        P("lat", "lon", None),
        P("lat", "lon"),
        P(None, "lat", "lon"),
        P("lat", "lon"),
        P(),
    )
    return jax.shard_map(
        on_device,
        mesh=mesh,
        in_specs=placed,
        out_specs=(P(None, "lat", "lon"), P(None, "lat", "lon"), P(None, "lat", "lon")),
        check_vma=False,
    )
```

```python
import functools

import jax
import jax.numpy as jnp
from jax import lax
from jax.experimental import pallas as pl
from jax.experimental.pallas import tpu as pltpu
from jax.sharding import PartitionSpec as P

ROWS = 4
LANES = 128
SPAN = 64
F32 = jnp.float32
BF16 = jnp.bfloat16


def iota(shape, dim):
    return lax.broadcasted_iota(jnp.int32, shape, dim)


def swap(block, axis, odd):
    count = lax.axis_size(axis)
    ends = [(i, i + 1) for i in range(odd, count - 1, 2)]
    if odd and axis == "lon":
        ends.append((count - 1, 0))
    return lax.ppermute(block, axis, ends + [(b, a) for a, b in ends])


def swaps(even_block, odd_block, axis):
    return swap(even_block, axis, 0), swap(odd_block, axis, 1)


def from_pole(block, ends):
    sectors = lax.axis_size("lon")
    pairs = [
        (source * sectors + s, band * sectors + (s + sectors // 2) % sectors)
        for source, band in ends
        for s in range(sectors)
    ]
    return lax.ppermute(block, ("lat", "lon"), pairs)


def from_far(block):
    last = lax.axis_size("lat") - 1
    return from_pole(block, ((0, 0), (last, last)))


def from_far_next(block):
    last = lax.axis_size("lat") - 1
    return from_pole(block, ((1, 0), (last - 1, last)))


def after(block, *others):
    return lax.optimization_barrier((block,) + others)[0]


def coded(depart_lists, tiles):
    bands, sectors = lax.axis_size("lat"), lax.axis_size("lon")
    band, sector = lax.axis_index("lat"), lax.axis_index("lon")
    wanted = depart_lists.transpose(1, 2, 0).reshape(1, -1)
    owner = wanted // tiles
    theirs = owner % sectors
    turn = jnp.where(theirs == (sector ^ 1), 1, 2)
    turn = jnp.where(theirs == (sector + sectors // 2) % sectors, 3, turn)
    turn = jnp.where(theirs == sector, 0, turn)
    source = owner // sectors
    place = jnp.where(source == band, 0, jnp.where(source == (band ^ 1), 1, 2))
    code = turn * SPAN + place * tiles + wanted % tiles
    return jnp.pad(code, ((0, 0), (0, LANES - code.shape[1])), constant_values=4 * SPAN)


def flat(rows):
    return pl.BlockSpec((rows, LANES), lambda g: (0, 0))


def ranks(member):
    before = (iota((LANES, LANES), 0) < iota((LANES, LANES), 1)).astype(BF16)
    ones = jnp.where(member, 1.0, 0.0).astype(BF16)
    return jnp.dot(ones, before, preferred_element_type=F32)


def pack_kernel(count, *refs):
    lists, (own, next_even, next_odd), outs, pick = refs[:count], refs[count : count + 3], refs[count + 3 : -1], refs[-1]

    @pl.when(pl.program_id(0) == 0)
    def _():
        sub = iota((8, LANES), 0)
        codes = jnp.where(sub == 0, lists[0][...], lists[1][...])
        if count > 2:
            far_codes = lists[2][0].astype(F32)[:8].astype(jnp.int32)
            codes = jnp.where(sub == 2, far_codes, codes)
        member = (codes >> 6) == sub + 1
        rank = jnp.where(member, ranks(member), -1.0)
        tile = ((codes & (SPAN - 1)) + 1).astype(F32)
        slot = (iota((64, LANES), 0) >> 2).astype(F32)
        row = (iota((64, 192), 0) & 3).astype(F32)
        col = iota((64, 192), 1).astype(F32)
        for d in range(count):
            hit = rank[d : d + 1] == slot
            held = jnp.sum(jnp.where(hit, tile[d : d + 1], 0.0), axis=1, keepdims=True) - 1.0
            pick[d * 64 : (d + 1) * 64, :] = jnp.where(col == held * 4.0 + row, 1.0, 0.0).astype(BF16)

    def pair(g, carry):
        pool = jnp.concatenate(
            [jnp.concatenate([ref[f] for ref in (own, next_even, next_odd)], axis=0) for f in (2 * g, 2 * g + 1)],
            axis=1,
        )
        got = jnp.dot(pick[...], pool, preferred_element_type=F32).astype(BF16)
        for d, out in enumerate(outs):
            for half in range(2):
                out[2 * g + half] = got[d * 64 : (d + 1) * 64, half * LANES : (half + 1) * LANES]
        return carry

    lax.fori_loop(0, 8, pair, 0, unroll=8)


def pack(lists, bands, blocks, of):
    levels, count = 16 * blocks, len(lists)
    source = pl.BlockSpec((16, 64, LANES), lambda g: (of(g), 0, 0))
    block = pl.BlockSpec((16, 64, LANES), lambda g: (g, 0, 0))
    rows = [flat(1)] * 2 + [pl.BlockSpec((1, 64, LANES), lambda g: (32, 0, 0))] * (count - 2)
    return pl.pallas_call(
        functools.partial(pack_kernel, count),
        grid=(blocks,),
        in_specs=rows + [source] * 3,
        out_specs=[block] * count,
        out_shape=[jax.ShapeDtypeStruct((levels, 64, LANES), BF16)] * count,
        scratch_shapes=[pltpu.VMEM((count * 64, 192), BF16)],
        compiler_params=pltpu.CompilerParams(vmem_limit_bytes=32 << 20),
        cost_estimate=pl.CostEstimate(
            flops=levels * 2 * 192 * 192 * LANES, bytes_accessed=levels * 5 * 64 * LANES * 2, transcendentals=0
        ),
        name="pack",
    )(*lists, *bands)


def set_gather(codes_ref, gather, far_slots):
    codes = jnp.broadcast_to(codes_ref[...], (8, LANES))
    turn = codes >> 6
    sub = iota((8, LANES), 0)
    rank = ranks(turn == sub)
    turn, tile = turn[:1], codes[:1] & (SPAN - 1)
    place = jnp.where(turn == 0, tile.astype(F32), -1.0)
    even_at, odd_at = (64.0, 48.0) if far_slots else (48.0, 64.0)
    place = jnp.where(turn == 1, even_at + rank[1:2], place)
    place = jnp.where(turn == 2, odd_at + rank[2:3], place)
    if far_slots:
        across = 80.0 + rank[3:4]
    else:
        across = ((tile & 15) + jnp.where(tile < 16, 80, 96)).astype(F32)
    place = jnp.where(turn == 3, across, place)
    row = iota((LANES, LANES), 0)
    mine = iota((LANES, LANES), 1) == (row & 15) + 16 * (row >> 6)
    place = jnp.sum(jnp.where(mine, place, 0.0), axis=1, keepdims=True)
    within = ((iota(gather.shape, 0) >> 4) & 3).astype(F32)
    col = iota(gather.shape, 1).astype(F32)
    gather[...] = jnp.where(col == place * 4.0 + within, 1.0, 0.0).astype(BF16)


def every_fourth(q):
    return pl.ds(q, 16, stride=4)


def set_weights(table, coef):
    for q in range(4):
        *points, offset = (table[m, every_fourth(q), :] for m in range(5))
        for r in range(8):
            value = jnp.zeros((16, LANES), F32)
            for m in range(4):
                if 0 <= r - m <= 4:
                    value = jnp.where(offset == float(r - m), points[m], value)
            coef[q * 8 + r] = value


def interpolate(gather, coef, first_pools, second_pools, first, second=None):
    second = first if second is None else second
    pool = jnp.concatenate(
        [
            jnp.concatenate([ref[f] for ref in pools], axis=0)
            for pools, f in ((first_pools, first), (second_pools, second))
        ],
        axis=1,
    )
    rows = jnp.dot(gather[...], pool, preferred_element_type=F32)
    out = []
    for q in range(4):
        sums = [None, None]
        for r in range(8):
            weight = coef[q * 8 + r]
            for h in range(2):
                term = weight * rows[r * 16 : (r + 1) * 16, h * LANES : (h + 1) * LANES]
                sums[h] = term if r == 0 else sums[h] + term
        out.append(sums)
    return out


def levels_block(of):
    return pl.BlockSpec((16, 64, LANES), lambda g: (of(g), 0, 0))


SMEM = pl.BlockSpec(memory_space=pltpu.SMEM)
VMEM = pl.BlockSpec(memory_space=pltpu.VMEM)
TABLE = pl.BlockSpec((5, 64, LANES), lambda g: (0, 0, 0))


def scratch(pool):
    return [
        pltpu.VMEM((LANES, 64 * pool), BF16), pltpu.VMEM((32, 16, LANES), F32), pltpu.VMEM((16, 64, LANES), F32)
    ]


def first_kernel(scale, codes, table, diag, *refs):
    middle, top = refs[0:7], refs[7:14]
    adv, rhs, cols, edge_even, edge_odd, gather, coef, tmp, own_up, own_down = refs[14:]
    set_gather(codes, gather, False)
    set_weights(table, coef)

    def level(l, carry):
        values = interpolate(gather, coef, middle, top, l)
        for q in range(4):
            tmp[l, every_fourth(q), :] = values[q][0]
            rhs[l, every_fourth(q), :] = values[q][1] + 0.5 * values[q][0]
        return carry

    lax.fori_loop(0, 16, level, 0, unroll=16)
    group = iota((64, LANES), 1) >> 2
    packed = jnp.where(group == 16, pltpu.roll(diag[...], 65, 1), 0.0)
    for l in range(16):
        adv[l] = tmp[l].astype(BF16)
        value = rhs[l] / (4.0 + diag[...] * scale[l])
        for ref, ends in ((own_up, (0, 1)), (own_down, (63, 62))):
            for place, r in enumerate(ends):
                ref[16 * place + l : 16 * place + l + 1, :] = value[r : r + 1]
        packed = jnp.where(group == l, pltpu.roll(value, 2 + 4 * l, 1), packed)
    cols[...] = packed
    for ref, r in ((own_up, 0), (own_down, 63)):
        ref[32:33, :] = diag[r : r + 1, :]
        ref[33:40, :] = jnp.ones((7, LANES), F32)
    up, down = own_up[...], own_down[...]
    even_band = lax.rem(lax.axis_index("lat"), 2) == 0
    edge_even[...] = jnp.where(even_band, down, up)
    edge_odd[...] = jnp.where(even_band, up, down)


def first_levels(scale, codes, table, diag, bands, slots, far):
    slab = jax.ShapeDtypeStruct((16, 64, LANES), F32)
    edge = jax.ShapeDtypeStruct((40, LANES), F32)
    whole = levels_block(lambda g: 0)
    pools, specs = [], []
    for half in range(2):
        pools += [*bands, *slots, *far]
        specs += [levels_block(lambda g, half=half: 2 + 2 * half)] * 3 + [levels_block(lambda g, half=half: half)] * 4
    return pl.pallas_call(
        first_kernel,
        grid=(1,),
        in_specs=[SMEM, flat(1), TABLE, flat(64)] + specs,
        out_specs=[levels_block(lambda g: 2), whole, flat(64)] + [flat(40)] * 2,
        out_shape=[
            jax.ShapeDtypeStruct((64, 64, LANES), BF16), slab, jax.ShapeDtypeStruct((64, LANES), F32)
        ] + [edge] * 2,
        scratch_shapes=scratch(7) + [pltpu.VMEM((40, LANES), F32)] * 2,
        compiler_params=pltpu.CompilerParams(vmem_limit_bytes=32 << 20),
        cost_estimate=pl.CostEstimate(flops=32 * 2 * 128 * 448 * 128, bytes_accessed=6 << 20, transcendentals=0),
        name="first_levels",
    )(scale, codes, table, diag, *pools)


def other_kernel(codes, table, *refs):
    pools, (start, adv, gather, coef, tmp) = refs[:6], refs[6:]

    @pl.when(pl.program_id(0) == 0)
    def _():
        set_gather(codes, gather, True)
        set_weights(table, coef)

    def pair(g, carry):
        values = interpolate(gather, coef, pools, pools, 2 * g, 2 * g + 1)
        for h in range(2):
            for q in range(4):
                tmp[2 * g + h, every_fourth(q), :] = values[q][h]
        return carry

    lax.fori_loop(0, 8, pair, 0, unroll=8)
    for f in range(16):
        adv[f] = tmp[f].astype(BF16)


def other_levels(codes, table, bands, slots, start):
    return pl.pallas_call(
        other_kernel,
        grid=(3,),
        in_specs=[flat(1), TABLE]
        + [levels_block(lambda g: g + g // 2)] * 3
        + [levels_block(lambda g: g)] * 3
        + [pl.BlockSpec(memory_space=pl.ANY)],
        out_specs=levels_block(lambda g: g + g // 2),
        out_shape=jax.ShapeDtypeStruct(start.shape, start.dtype),
        scratch_shapes=scratch(6),
        input_output_aliases={8: 0},
        compiler_params=pltpu.CompilerParams(vmem_limit_bytes=32 << 20),
        cost_estimate=pl.CostEstimate(flops=48 * 2 * 128 * 448 * 128, bytes_accessed=6 << 20, transcendentals=0),
        name="other_levels",
    )(codes, table, *bands, *slots, start)


def sum_kernel(scale, rhs, diag, cols, cols_even, cols_odd, edge_even, edge_odd, n0, n1, sums, rowsums):
    lane = iota((64, LANES), 1)
    even_band = lax.rem(lax.axis_index("lat"), 2) == 0
    even_sector = lax.rem(lax.axis_index("lon"), 2) == 0
    even, odd = edge_even[...], edge_odd[...]
    above, below = jnp.where(even_band, odd, even), jnp.where(even_band, even, odd)
    even, odd = cols_even[...], cols_odd[...]
    left, right = jnp.where(even_sector, odd, even), jnp.where(even_sector, even, odd)
    spread = jnp.zeros((1, LANES), F32)
    column = jnp.zeros((16, LANES), F32)
    for l in range(16):
        spread = jnp.where((lane[:1] >> 2) == l, scale[l], spread)
        column = jnp.where(iota((16, LANES), 0) == l, scale[l], column)
    row16, lane16 = iota((16, LANES), 0), lane[:16]

    west_even, west_odd = left[64:80, LANES - 1 : LANES], left[80:96, LANES - 1 : LANES]
    east_even, east_odd = right[64:80, 0:1], right[80:96, 0:1]
    corners = [
        [jnp.where(even_band, west_odd, west_even), jnp.where(even_band, east_odd, east_even)],
        [jnp.where(even_band, west_even, west_odd), jnp.where(even_band, east_even, east_odd)],
    ]

    def spread_corner(column, which):
        return jnp.sum(jnp.where(lane16 == 4 * row16 + which, column, 0.0), axis=0, keepdims=True)

    def rim_row(edge, inner, west, east):
        near, second, flag = edge[0:16, :], edge[16:32, :], edge[33:34, :]
        beside = jnp.where(lane16 == 0, west, pltpu.roll(near, 1, 1))
        beside = beside + jnp.where(lane16 == LANES - 1, east, pltpu.roll(near, LANES - 1, 1))
        return flag * (second + inner + beside) / (4.0 + edge[32:33, :] * column)

    def own_row(r):
        rows = jnp.concatenate([rhs[l, r : r + 1, :] for l in range(16)], axis=0)
        return rows / (4.0 + diag[r : r + 1, :] * column)

    top, bottom = rim_row(above, own_row(0), *corners[0]), rim_row(below, own_row(63), *corners[1])

    def rim_col(edge, side, which, toward, diag_lane):
        values = edge[0:64]
        first, last = (spread_corner(pair[side], which) for pair in corners)
        up = jnp.concatenate([first, values[:-1]], axis=0)
        down = jnp.concatenate([values[1:], last], axis=0)
        outer = pltpu.roll(values, toward % LANES, 1)
        inner = pltpu.roll(cols[...], -toward % LANES, 1)
        coef = 4.0 + values[:, diag_lane : diag_lane + 1] * spread
        return (up + down + outer + inner) / coef

    west = rim_col(left, 0, 1, 1, 64)
    east = rim_col(right, 1, 2, -1, 65)

    def beside(value, west_col, east_col, upper, lower):
        total = jnp.where(lane == 0, west_col, pltpu.roll(value, 1, 1))
        total = total + jnp.where(lane == LANES - 1, east_col, pltpu.roll(value, LANES - 1, 1))
        total = total + jnp.concatenate([upper, value[:-1]], axis=0)
        return total + jnp.concatenate([value[1:], lower], axis=0)

    for l in range(16):
        start = rhs[l]
        inverse = 1.0 / (4.0 + diag[...] * scale[l])
        value = start * inverse
        around = beside(
            value, left[0:64, 4 * l + 1 : 4 * l + 2], right[0:64, 4 * l + 2 : 4 * l + 3], above[l : l + 1, :], below[l : l + 1, :]
        )
        n0[l] = around
        again = around * inverse
        second = beside(
            again, west[:, 4 * l + 1 : 4 * l + 2], east[:, 4 * l + 2 : 4 * l + 3], top[l : l + 1], bottom[l : l + 1]
        )
        n1[l] = second
        for k, term in enumerate((start * value, start * again, around * again, second * again)):
            part = term[0:8]
            for j in range(1, 8):
                part = part + term[8 * j : 8 * j + 8]
            rowsums[k * 16 + l : k * 16 + l + 1, :] = jnp.sum(part, axis=0, keepdims=True)
    total = jnp.sum(rowsums[...], axis=1, keepdims=True)
    packed = jnp.sum(jnp.where(lane == iota((64, LANES), 0), total, 0.0), axis=0, keepdims=True)
    for j in range(sums.shape[0]):
        sums[j] = packed


def level_sums(scale, rhs, diag, cols, cols_rim, edges):
    slab = jax.ShapeDtypeStruct((16, 64, LANES), F32)
    return pl.pallas_call(
        sum_kernel,
        in_specs=[SMEM] + [VMEM] * 7,
        out_specs=[VMEM] * 3,
        out_shape=[slab, slab, jax.ShapeDtypeStruct((lax.axis_size("lat"), 1, LANES), F32)],
        scratch_shapes=[pltpu.VMEM((64, LANES), F32)],
        compiler_params=pltpu.CompilerParams(vmem_limit_bytes=60 << 20),
        cost_estimate=pl.CostEstimate(flops=1 << 22, bytes_accessed=2 << 20, transcendentals=0),
        name="level_sums",
    )(scale, rhs, diag, cols, *cols_rim, *edges)


def last_kernel(scale, parts, rhs, diag, n0, n1, pressure, residual):
    total = parts[0]
    for j in range(1, parts.shape[0]):
        total = total + parts[j]
    total = jnp.broadcast_to(total, (8, LANES))
    lane, row = iota((8, LANES), 1), iota((8, LANES), 0)

    def of(k, half):
        return jnp.sum(jnp.where(lane == 16 * k + 8 * half + row, total, 0.0), axis=1, keepdims=True)

    half = pl.program_id(0)
    s0, s1, s2, s3 = (of(k, half) for k in range(4))
    curve = s0 - s1
    step = s0 / curve
    keep = -s1 / curve
    norm = keep * keep * s0 + 2.0 * keep * step * s1 + step * step * s2
    ratio = norm / s0
    bend = norm - (keep * keep * s1 + 2.0 * keep * step * s2 + step * step * s3)
    other = norm / (bend - ratio * ratio * curve)
    along = other * (keep + ratio)
    across = other * step
    fit_z, fit_p = step + along, across
    fit_r, fit_n0, fit_n1 = keep - along, step + along - across, across
    for s in range(8):
        at = lambda column: column[s : s + 1]
        inverse = 1.0 / (4.0 + diag[...] * scale[8 * half + s])
        start, around = rhs[s], n0[s]
        pressure[s] = (at(fit_z) * start + at(fit_p) * around) * inverse
        residual[s] = at(fit_r) * start + at(fit_n0) * around + at(fit_n1) * n1[s]


def last_step(scale, parts, rhs, diag, n0, n1):
    slab = jax.ShapeDtypeStruct((16, 64, LANES), F32)
    block = pl.BlockSpec((8, 64, LANES), lambda g: (g, 0, 0))
    return pl.pallas_call(
        last_kernel,
        grid=(2,),
        in_specs=[SMEM, pl.BlockSpec(parts.shape, lambda g: (0, 0, 0)), block, flat(64), block, block],
        out_specs=[block] * 2,
        out_shape=[slab, slab],
        input_output_aliases={2: 1, 4: 0},
        compiler_params=pltpu.CompilerParams(vmem_limit_bytes=60 << 20),
        cost_estimate=pl.CostEstimate(flops=1 << 21, bytes_accessed=3 << 20, transcendentals=0),
        name="last_step",
    )(scale, parts, rhs, diag, n0, n1)


def exchange(parts, axis):
    return lax.all_to_all(parts, axis, split_axis=0, concat_axis=0, tiled=True)


def on_device(fields, depart_lists, stencil_offsets, interp_weights, diag_coef, level_scale):
    tiles = depart_lists.shape[0]
    codes = coded(depart_lists, tiles)
    bands = (fields,) + swaps(fields, fields, "lat")
    lists = swaps(codes, codes, "lon")
    rows = jnp.broadcast_to(codes.astype(BF16)[None], (1, 64, LANES))
    first = after(jnp.concatenate([fields[32:48], fields[64:80], rows], axis=0), lists[0])
    first_far = (from_far(first), from_far_next(first))
    first_out = pack(lists, bands, 2, lambda g: 2 + 2 * g)
    first_slots = swaps(*first_out, "lon")
    later = after(lists[0], *first_out, *first_far)
    offsets = after(stencil_offsets, *first_out)
    table = jnp.concatenate([interp_weights, offsets.astype(F32)[None]], axis=0)
    *other_out, other_far = pack((later, lists[1], first_far[0]), bands, 3, lambda g: g + g // 2)
    other_slots = swaps(*other_out, "lon")
    first_slots = (after(first_slots[0], *other_out), first_slots[1])
    adv, rhs, cols, *edges = first_levels(
        level_scale, codes, table, diag_coef, bands, first_slots, first_far
    )
    edges = swaps(*edges, "lat")
    rim = jnp.concatenate([cols, edges[0][:16], edges[1][:16]], axis=0)
    cols_rim = swaps(rim, rim, "lon")
    other_far = from_far(after(other_far, *cols_rim))
    n0, n1, parts = level_sums(level_scale, rhs, diag_coef, cols, cols_rim, edges)
    parts = jnp.sum(exchange(parts, "lat"), axis=0)
    parts = exchange(jnp.broadcast_to(parts[None], (lax.axis_size("lon"),) + parts.shape), "lon")
    adv = other_levels(codes, table, bands, (other_slots[1], other_slots[0], other_far), adv)
    parts = after(parts, adv)
    pressure, residual = last_step(level_scale, parts, rhs, diag_coef, n0, n1)
    return (adv, pressure, residual)


def solution(mesh):
    placed = (
        P(None, "lat", "lon"),
        P("lat", "lon", None),
        P("lat", "lon"),
        P(None, "lat", "lon"),
        P("lat", "lon"),
        P(),
    )
    return jax.shard_map(
        on_device,
        mesh=mesh,
        in_specs=placed,
        out_specs=(P(None, "lat", "lon"), P(None, "lat", "lon"), P(None, "lat", "lon")),
        check_vma=False,
    )
```
